128 devices in a mesh: row: 16 (over z, y), col: 8 (over x, core).
Axes of the slice: x: 4, y: 4, z: 4, core: 2. Of those that a mesh axis runs over, the one named last changes fastest.
Arguments:
- profile_representation: bfloat16 [256, 768, 256], P('col', 'row'), may hold values from -6 to 6
- couple_embedding: bfloat16 [768, 768, 128], P('row', 'col'), may hold values from -6 to 6
- loss_sensitivity_pair: bfloat16 [768, 768, 128], P('row', 'col'), may hold values from -6 to 6
- former_mapping_weights: bfloat16 [256, 32], replicated, may hold values from -0.375 to 0.375
- latter_mapping_weights: bfloat16 [256, 32], replicated, may hold values from -0.375 to 0.375
- tensor_mixing_weights: bfloat16 [1024, 128], replicated, may hold values from -3 to 3
- expand_silu_matrix: bfloat16 [128, 512], replicated, may hold values from -0.5 to 0.5
- shrink_silu_matrix: bfloat16 [512, 128], replicated, may hold values from -0.25 to 0.25
Outputs:
- pairwise_output: bfloat16 [768, 768, 128], P(('row', 'col'))
- pairwise_gradient: bfloat16 [768, 768, 128], P('row', 'col')
- profile_slope_field: bfloat16 [256, 768, 256], P('col', 'row')
The draws below stay inside these ranges and needn't reach their ends.
All inputs are finite; a program needn't handle non-finite values.
Results may differ from the reference program's by a relative error of at most 0.023.
Values may be sent and summed in bfloat16 or wider, within the bound.
A program may use at most 128 MiB of HBM per device.

```python
import math
import jax
import jax.numpy as jnp
from jax import lax

PROFILE_CHANNELS = 256
DUAL_CHANNELS = 128
MAPPED_CHANNELS = 32
HIDDEN_CH = 512
HOMOLOGUE_TALLY = 256
COMPLEX_SIZE = 768


def steps_of(stream_key, shape, split, smallest, largest):
    gain = 1.0
    for position, shards_of in split:
        steps = jax.random.uniform(jax.random.fold_in(jax.random.fold_in(stream_key, 6), position), (shards_of,), jnp.float32, smallest / len(split), largest / len(split))
        gain = gain * jnp.repeat(jnp.exp(steps), shape[position] // shards_of).reshape((-1,) + (1,) * (len(shape) - 1 - position))
    return gain


def noise(key, dims, spread, reach, cuts=(), held_as=jnp.bfloat16):
    entries = jax.random.normal(key, dims, jnp.float32) * spread
    if len(cuts) > 0:
        entries = steps_of(key, dims, cuts, -0.22, 0.18) * entries
    return jnp.clip(entries, min=-reach, max=reach).astype(held_as)


def setup_inputs(seed: int = 0) -> dict:
    keys = jax.random.split(jax.random.key(seed), 9)
    return {
        "profile_representation": noise(keys[0], (HOMOLOGUE_TALLY, COMPLEX_SIZE, PROFILE_CHANNELS), 1.0, 6.0, ((0, 8), (1, 16))),
        "couple_embedding": noise(keys[1], (COMPLEX_SIZE, COMPLEX_SIZE, DUAL_CHANNELS), 1.0, 6.0, ((0, 16), (1, 8))),
        "loss_sensitivity_pair": noise(keys[2], (COMPLEX_SIZE, COMPLEX_SIZE, DUAL_CHANNELS), 1.0, 6.0, ((0, 16), (1, 8))),
        "former_mapping_weights": noise(keys[3], (PROFILE_CHANNELS, MAPPED_CHANNELS), PROFILE_CHANNELS ** -0.5, 0.375),
        "latter_mapping_weights": noise(keys[4], (PROFILE_CHANNELS, MAPPED_CHANNELS), PROFILE_CHANNELS ** -0.5, 0.375),
        "tensor_mixing_weights": noise(keys[5], (MAPPED_CHANNELS * MAPPED_CHANNELS, DUAL_CHANNELS), (max(MAPPED_CHANNELS * MAPPED_CHANNELS // HOMOLOGUE_TALLY, 1)) ** -0.5, 3.0),
        "expand_silu_matrix": noise(keys[6], (DUAL_CHANNELS, HIDDEN_CH), DUAL_CHANNELS ** -0.5, 0.5),
        "shrink_silu_matrix": noise(keys[7], (HIDDEN_CH, DUAL_CHANNELS), HIDDEN_CH ** -0.5, 0.25),
    }


epsilon = 1e-05

def perform_rescaling(values):
    center = values - lax.optimization_barrier(jnp.mean(values, axis=-1, keepdims=True))
    inverse_deviation = lax.rsqrt(lax.optimization_barrier(jnp.mean(center * center, axis=-1, keepdims=True)) + epsilon)
    return (center * inverse_deviation, inverse_deviation)

def rescaling_reverse_pass(incoming_gradient, centered_normed, inverse_deviation):
    outer_mean_gradient = lax.optimization_barrier(jnp.mean(incoming_gradient, axis=-1, keepdims=True))
    outer_mean_projected = lax.optimization_barrier(jnp.mean(incoming_gradient * centered_normed, axis=-1, keepdims=True))
    return (incoming_gradient - outer_mean_gradient - centered_normed * outer_mean_projected) * inverse_deviation

def reference(profile_representation, couple_embedding, loss_sensitivity_pair, former_mapping_weights, latter_mapping_weights, tensor_mixing_weights, expand_silu_matrix, shrink_silu_matrix):
    multiplier = 1.0 / HOMOLOGUE_TALLY
    whitened_profile_values, profile_unit_scaler = perform_rescaling(profile_representation.astype(jnp.float32))
    profile_rescaled = whitened_profile_values.astype(jnp.bfloat16).reshape(-1, PROFILE_CHANNELS)
    former_mapped = jnp.dot(profile_rescaled, former_mapping_weights, preferred_element_type=jnp.float32).astype(jnp.bfloat16)
    former_mapped = former_mapped.reshape(HOMOLOGUE_TALLY, COMPLEX_SIZE, MAPPED_CHANNELS)
    latter_mapped = jnp.dot(profile_rescaled, latter_mapping_weights, preferred_element_type=jnp.float32).astype(jnp.bfloat16)
    latter_mapped = latter_mapped.reshape(HOMOLOGUE_TALLY, COMPLEX_SIZE, MAPPED_CHANNELS)
    right_wide = latter_mapped.astype(jnp.float32)
    block = math.gcd(COMPLEX_SIZE, 16)
    count = COMPLEX_SIZE // block

    def step(carry, index):
        start = (index * block).astype(jnp.int32)
        pair_rows = lax.dynamic_slice_in_dim(couple_embedding, start, block, 0)
        cot_rows = lax.dynamic_slice_in_dim(loss_sensitivity_pair, start, block, 0)
        left_rows = lax.dynamic_slice_in_dim(former_mapped, start, block, 1).astype(jnp.float32)
        outer = jnp.einsum('sip,sjq->ijpq', left_rows, right_wide) * multiplier
        outer = outer.astype(jnp.bfloat16).reshape(block * COMPLEX_SIZE, MAPPED_CHANNELS * MAPPED_CHANNELS)
        update = jnp.dot(outer, tensor_mixing_weights, preferred_element_type=jnp.float32)
        mid = (pair_rows.reshape(block * COMPLEX_SIZE, DUAL_CHANNELS).astype(jnp.float32) + update).astype(jnp.bfloat16)
        transition_hidden = mid.astype(jnp.float32)
        pairwise_centered_normed, pairwise_inverse_deviation = perform_rescaling(transition_hidden)
        activation_input = jnp.dot(pairwise_centered_normed.astype(jnp.bfloat16), expand_silu_matrix, preferred_element_type=jnp.float32)
        hidden = jax.nn.silu(activation_input).astype(jnp.bfloat16)
        out_rows = (transition_hidden + jnp.dot(hidden, shrink_silu_matrix, preferred_element_type=jnp.float32)).astype(jnp.bfloat16)
        cotangent_flat = cot_rows.reshape(block * COMPLEX_SIZE, DUAL_CHANNELS)
        hidden_grad = jnp.dot(cotangent_flat, shrink_silu_matrix.T, preferred_element_type=jnp.float32)
        sigma = jax.nn.sigmoid(activation_input)
        pre_grad = (hidden_grad * sigma * (1.0 + activation_input * (1.0 - sigma))).astype(jnp.bfloat16)
        normed_gradient = jnp.dot(pre_grad, expand_silu_matrix.T, preferred_element_type=jnp.float32)
        gradient_rows = (cotangent_flat.astype(jnp.float32) + rescaling_reverse_pass(normed_gradient, pairwise_centered_normed, pairwise_inverse_deviation)).astype(jnp.bfloat16)
        outer_grad = jnp.dot(gradient_rows, tensor_mixing_weights.T, preferred_element_type=jnp.float32).astype(jnp.bfloat16)
        outer_grad = outer_grad.reshape(block, COMPLEX_SIZE, MAPPED_CHANNELS, MAPPED_CHANNELS).astype(jnp.float32)
        left_term = jnp.einsum('ijpq,sjq->sip', outer_grad, right_wide) * multiplier
        right_term = jnp.einsum('ijpq,sip->sjq', outer_grad, left_rows) * multiplier
        outs = (out_rows.reshape(block, COMPLEX_SIZE, DUAL_CHANNELS), gradient_rows.reshape(block, COMPLEX_SIZE, DUAL_CHANNELS), left_term)
        return (carry + right_term, outs)
    initial_accumulator = jnp.zeros((HOMOLOGUE_TALLY, COMPLEX_SIZE, MAPPED_CHANNELS), jnp.float32)
    latter_mapped_slope, (out_blocks, grad_blocks, former_pieces) = lax.scan(step, initial_accumulator, jnp.arange(count, dtype=jnp.int32))
    pairwise_output = out_blocks.reshape(COMPLEX_SIZE, COMPLEX_SIZE, DUAL_CHANNELS)
    pairwise_gradient = grad_blocks.reshape(COMPLEX_SIZE, COMPLEX_SIZE, DUAL_CHANNELS)
    former_mapped_slope = jnp.transpose(former_pieces, (1, 0, 2, 3)).reshape(HOMOLOGUE_TALLY * COMPLEX_SIZE, MAPPED_CHANNELS)
    rescaled_profile = jnp.dot(former_mapped_slope, former_mapping_weights.astype(jnp.float32).T, precision=lax.Precision.HIGHEST)
    rescaled_profile = rescaled_profile + jnp.dot(latter_mapped_slope.reshape(HOMOLOGUE_TALLY * COMPLEX_SIZE, MAPPED_CHANNELS), latter_mapping_weights.astype(jnp.float32).T, precision=lax.Precision.HIGHEST)
    profile_slope_field = rescaling_reverse_pass(rescaled_profile.reshape(HOMOLOGUE_TALLY, COMPLEX_SIZE, PROFILE_CHANNELS), whitened_profile_values, profile_unit_scaler).astype(jnp.bfloat16)
    return (pairwise_output, pairwise_gradient, profile_slope_field)
```

```python
import functools

import jax
import jax.numpy as jnp
from jax import lax
from jax.experimental import pallas as pl
from jax.experimental.pallas import tpu as pltpu
from jax.sharding import PartitionSpec as P

MESH = pl.DeviceIdType.MESH
EPS = 1e-05
F32 = jnp.float32
BF16 = jnp.bfloat16

ROWS, COLS = 16, 8
S, SL = 256, 32
I, J, JP = 48, 96, 128
Q = 32
C, H, CH = 128, 512, 256
SK = S // ROWS
G8 = Q // 4
PK = 3 * G8 * 128
FULL = Q * JP
IB = I // COLS
SLABS = [4 * (k // 3) + k % 3 for k in range(3 * G8)] + [4 * g + 3 for g in range(G8)]


def dot(a, b):
    return jnp.dot(a, b, preferred_element_type=F32)


def dot_nt(a, b):
    return lax.dot_general(a, b, (((1,), (1,)), ((), ())), preferred_element_type=F32)


def eye(n, m=None):
    m = n if m is None else m
    i = lax.broadcasted_iota(jnp.int32, (n, m), 0)
    j = lax.broadcasted_iota(jnp.int32, (n, m), 1)
    return jnp.where(i == j, 1.0, 0.0).astype(BF16)


def lanes(shape):
    return lax.broadcasted_iota(jnp.int32, shape, 1)


def roll(x, shift):
    return pltpu.roll(x, shift, 1)


def pack4(q0, q1, q2, q3):
    ln = lanes(q0.shape)
    return (
        jnp.where(ln < 96, q0, roll(q3, 96)),
        jnp.where(ln < 96, q1, roll(q3, 64)),
        jnp.where(ln < 96, q2, roll(q3, 32)),
    )


def unpack_fourth(t0, t1, t2):
    ln = lanes(t0.shape)
    return jnp.where(ln < 32, roll(t0, 32), jnp.where(ln < 64, roll(t1, 64), roll(t2, 96)))


def kernel(
    x_ref, pair_ref, loss_ref, f_ref, g_ref, w_ref, e_ref, s_ref,
    out_ref, grad_ref, slope_ref,
    xhat, rstd, proj, tq, lall, lt, rhop, rin, rm, xs, ogs, obuf,
    wf32, wf, wt, et, st, lgs, lgt, lgin, rgp, rgin, rh, rhin, hg,
    hop_s, hop_r, lga_s, lga_r, rga_s, rga_r, a2a_s, a2a_r, lrs_s, lrs_r, rrs_s, rrs_r, hop2_s, hop2_r,
):
    r = lax.axis_index("row")
    c = lax.axis_index("col")
    half = lax.rem(r, 2)
    across = lax.div(r, 2)

    barrier = pltpu.get_barrier_semaphore()

    def greet_row(d, _):
        pl.semaphore_signal(barrier, inc=1, device_id=(lax.rem(r + d, ROWS), c), device_id_type=MESH)
        return 0

    def greet_col(d, _):
        pl.semaphore_signal(barrier, inc=1, device_id=(r, lax.rem(c + d, COLS)), device_id_type=MESH)
        return 0

    lax.fori_loop(1, ROWS, greet_row, 0)
    lax.fori_loop(1, COLS, greet_col, 0)
    own = [jnp.logical_and(across == c, half == t) for t in range(2)]
    for t in range(2):
        @pl.when(jnp.logical_not(own[t]))
        def _():
            pl.semaphore_signal(barrier, inc=1, device_id=(2 * c + t, across), device_id_type=MESH)

    iden = eye(C)
    ln128 = lanes((SL, 128))
    tile4 = jnp.where(
        lax.rem(lax.broadcasted_iota(jnp.int32, (Q, 128), 1), Q)
        == lax.broadcasted_iota(jnp.int32, (Q, 128), 0), 1.0, 0.0).astype(BF16)
    f4 = dot(f_ref[...], tile4).astype(BF16)
    gt = dot_nt(eye(Q), g_ref[...]).astype(BF16)
    tq[...] = jnp.zeros_like(tq)

    def project(b, _):
        rows = 4 * I
        at = pl.multiple_of(b * rows, rows)
        x = x_ref[pl.ds(b * 4, 4)].reshape(rows, CH).astype(F32)
        center = x - jnp.mean(x, axis=-1, keepdims=True)
        inv = lax.rsqrt(jnp.mean(center * center, axis=-1, keepdims=True) + EPS)
        xn = center * inv
        xhat[pl.ds(at, rows), :] = xn
        rstd[pl.ds(at, rows), :] = inv
        xb = xn.astype(BF16)
        proj[pl.ds(at, rows), :] = dot(xb, f4)
        for k in range(4):
            to = pl.multiple_of((b * 4 + k) * Q, Q)
            tq[pl.ds(to, Q), 0:I] = dot_nt(gt, xb[k * I:(k + 1) * I])
        return 0

    lax.fori_loop(0, SL // 4, project, 0)

    mine = pl.ds(pl.multiple_of(c * SL, SL), SL)
    for qp in range(Q // 2):
        even = tq[pl.ds(2 * qp, SL, stride=Q), :]
        odd = tq[pl.ds(2 * qp + 1, SL, stride=Q), :]
        rhop[qp] = jnp.where(ln128 < 64, even, roll(odd, 64)).astype(BF16)
    for g in range(I // 4):
        parts = [proj[pl.ds(4 * g + a, SL, stride=I), :] for a in range(4)]
        tile = jnp.where(ln128 < 32, parts[0], jnp.where(ln128 < 64, parts[1],
                         jnp.where(ln128 < 96, parts[2], parts[3])))
        lall[mine, g * 128:(g + 1) * 128] = tile.astype(BF16)

    pl.semaphore_wait(barrier, ROWS + COLS - (across == c).astype(jnp.int32))

    def hop_remote(src, dst, t, ss, rs):
        return pltpu.make_async_remote_copy(
            src_ref=src, dst_ref=dst, send_sem=ss.at[t], recv_sem=rs,
            device_id=(2 * c + t, across), device_id_type=MESH)

    def hop_start(src, dst, t, ss, rs):
        @pl.when(own[t])
        def _():
            pltpu.make_async_copy(src, dst, rs).start()

        @pl.when(jnp.logical_not(own[t]))
        def _():
            hop_remote(src, dst, t, ss, rs).start()

    def hop_wait(src, dst, t, ss, rs):
        @pl.when(own[t])
        def _():
            pltpu.make_async_copy(src, dst, rs).wait()

        @pl.when(jnp.logical_not(own[t]))
        def _():
            hop_remote(src, dst, t, ss, rs).wait_recv()

    def hop_sent(src, dst, t, ss, rs):
        @pl.when(jnp.logical_not(own[t]))
        def _():
            hop_remote(src, dst, t, ss, rs).wait_send()

    for t in range(2):
        hop_start(rhop.at[:, pl.ds(SK * t, SK), :], rin.at[half], t, hop_s, hop_r.at[half])

    def l_copy(d):
        return pltpu.make_async_remote_copy(
            src_ref=lall.at[mine], dst_ref=lall.at[mine], send_sem=lga_s.at[d], recv_sem=lga_r.at[d],
            device_id=(r, lax.rem(c + d, COLS)), device_id_type=MESH)

    def l_start(d, _):
        l_copy(d).start()
        return 0

    lax.fori_loop(1, COLS, l_start, 0)

    for t in range(2):
        hop_wait(rhop.at[:, pl.ds(SK * t, SK), :], rin.at[t], t, hop_s, hop_r.at[t])

    ln16 = lanes((SK, 128))
    here = pl.ds(pl.multiple_of(r * SK, SK), SK)
    for g in range(G8):
        tiles = []
        for k in range(2):
            a = rin[0, 2 * g + k].astype(F32)
            b = rin[1, 2 * g + k].astype(F32)
            tiles.append(jnp.where(ln16 < 48, a, roll(b, 48)))
            tiles.append(jnp.where(ln16 < 48, roll(a, 64), roll(b, 112)))
        for k, tile in enumerate(pack4(*tiles)):
            rm[here, (3 * g + k) * 128:(3 * g + k + 1) * 128] = tile.astype(BF16)

    def r_copy(d):
        return pltpu.make_async_remote_copy(
            src_ref=rm.at[here, pl.ds(0, PK)], dst_ref=rm.at[here, pl.ds(0, PK)],
            send_sem=rga_s.at[d], recv_sem=rga_r.at[d],
            device_id=(lax.rem(r + d, ROWS), c), device_id_type=MESH)

    def r_start(d, _):
        r_copy(d).start()
        return 0

    lax.fori_loop(1, ROWS, r_start, 0)

    wf32[...] = w_ref[...].astype(F32)
    for k, q in enumerate(SLABS):
        wf[k * Q:(k + 1) * Q, :] = wf32[pl.ds(q, Q, stride=Q), :].astype(BF16)
    wt[...] = dot_nt(iden, wf[...]).astype(BF16)
    st[...] = dot_nt(iden, s_ref[...]).astype(BF16)
    et[...] = dot_nt(eye(H), e_ref[...]).astype(BF16)

    def l_wait(d, _):
        l_copy(d).wait_recv()
        return 0

    lax.fori_loop(1, COLS, l_wait, 0)
    e256 = eye(S)
    for k in range(I * Q // S):
        lt[k * S:(k + 1) * S, :] = dot_nt(e256, lall[:, k * S:(k + 1) * S]).astype(BF16)

    def r_wait(d, _):
        r_copy(d).wait_recv()
        return 0

    lax.fori_loop(1, ROWS, r_wait, 0)
    for g in range(G8):
        t0, t1, t2 = [rm[:, (3 * g + k) * 128:(3 * g + k + 1) * 128].astype(F32) for k in range(3)]
        rm[:, (3 * G8 + g) * 128:(3 * G8 + g + 1) * 128] = unpack_fourth(t0, t1, t2).astype(BF16)

    def a2a_copy(t):
        to = lax.rem(c + 1 + t, COLS)
        return pltpu.make_async_remote_copy(
            src_ref=obuf.at[pl.ds(to * IB, IB)], dst_ref=out_ref.at[:, pl.ds(pl.multiple_of(c * J, J), J), :],
            send_sem=a2a_s.at[t], recv_sem=a2a_r.at[t], device_id=(r, to), device_id_type=MESH)

    def own_copy():
        return pltpu.make_async_copy(
            obuf.at[pl.ds(c * IB, IB)], out_ref.at[:, pl.ds(pl.multiple_of(c * J, J), J), :],
            a2a_s.at[COLS - 1])

    pad = jnp.zeros((JP - J, C), BF16)
    scale = 1.0 / S

    def block(t, _):
        ib = lax.rem(c + 1 + t, COLS)
        ip = pl.ds(pl.multiple_of(ib * (IB * Q), IB * Q), IB * Q)
        ltb = lt[ip, :]
        for ch in range(8):
            d = dot(ltb, rm[:, ch * 512:(ch + 1) * 512]).astype(BF16)
            for k in range(4):
                slab = ch * 4 + k
                for i in range(IB):
                    xs[slab * Q:(slab + 1) * Q, i * JP:(i + 1) * JP] = d[i * Q:(i + 1) * Q, k * 128:(k + 1) * 128]
        for half_block in range(IB // 2):
            i0 = ib * IB + 2 * half_block
            ls = slice(half_block * 256, half_block * 256 + 256)
            upd = dot(wt[...], xs[:, ls]) * scale
            pr = jnp.concatenate([pair_ref[i0], pad, pair_ref[i0 + 1], pad], axis=0)
            lo = jnp.concatenate([loss_ref[i0], pad, loss_ref[i0 + 1], pad], axis=0)
            mid = (dot_nt(iden, pr) + upd).astype(BF16).astype(F32)
            center = mid - jnp.mean(mid, axis=0, keepdims=True)
            inv = lax.rsqrt(jnp.mean(center * center, axis=0, keepdims=True) + EPS)
            xn = center * inv
            pre = dot(et[...], xn.astype(BF16))
            hgr = dot_nt(s_ref[...], lo)
            sg = 0.5 * jnp.tanh(0.5 * pre) + 0.5
            hid = pre * sg
            pgr = (hgr * (sg + hid * (1.0 - sg))).astype(BF16)
            outb = (mid + dot(st[...], hid.astype(BF16))).astype(BF16)
            hatg = dot(e_ref[...], pgr)
            m1 = jnp.mean(hatg, axis=0, keepdims=True)
            m2 = jnp.mean(hatg * xn, axis=0, keepdims=True)
            gb = (dot_nt(iden, lo) + (hatg - m1 - xn * m2) * inv).astype(BF16)
            for i in range(2):
                sl = slice(i * JP, (i + 1) * JP)
                obuf[i0 + i] = dot_nt(iden[0:J], outb[:, sl]).astype(BF16)
                grad_ref[i0 + i] = dot_nt(iden[0:J], gb[:, sl]).astype(BF16)
            og = dot(wf[...], gb).astype(BF16)
            for i in range(2):
                to = pl.ds(pl.multiple_of((i0 + i) * Q, Q), Q)
                for k in range(Q):
                    ogs[to, k * 128:(k + 1) * 128] = og[k * Q:(k + 1) * Q, i * JP:(i + 1) * JP]

        @pl.when(t < COLS - 1)
        def _():
            a2a_copy(t).start()

        @pl.when(t == COLS - 1)
        def _():
            own_copy().start()

        lgs[ip, :] = dot_nt(ogs[ip, :], rm[...]).astype(BF16)
        return 0

    lax.fori_loop(0, COLS, block, 0)

    for k in range(I * Q // S):
        lgt[:, k * S:(k + 1) * S] = dot_nt(e256, lgs[k * S:(k + 1) * S, :]).astype(BF16)

    def lrs_copy(d):
        to = lax.rem(c + d, COLS)
        return pltpu.make_async_remote_copy(
            src_ref=lgt.at[pl.ds(pl.multiple_of(to * SL, SL), SL)], dst_ref=lgin.at[d],
            send_sem=lrs_s.at[d], recv_sem=lrs_r.at[d], device_id=(r, to), device_id_type=MESH)

    def lrs_start(d, _):
        lrs_copy(d).start()
        return 0

    lax.fori_loop(1, COLS, lrs_start, 0)

    for g in range(0, G8, 2):
        a = dot(lall[...], ogs[:, 3 * g * 128:(3 * g + 6) * 128])
        b = dot(lall[...], ogs[:, (3 * G8 + g) * 128:(3 * G8 + g + 2) * 128])
        for k in range(2):
            tiles = pack4(*[a[:, (3 * k + m) * 128:(3 * k + m + 1) * 128] for m in range(3)],
                          b[:, k * 128:(k + 1) * 128])
            for m in range(3):
                at = (3 * (g + k) + m) * 128
                rgp[:, at:at + 128] = tiles[m].astype(BF16)

    def rrs_copy(d):
        to = lax.rem(r + d, ROWS)
        return pltpu.make_async_remote_copy(
            src_ref=rgp.at[pl.ds(pl.multiple_of(to * SK, SK), SK)], dst_ref=rgin.at[d],
            send_sem=rrs_s.at[d], recv_sem=rrs_r.at[d], device_id=(to, c), device_id_type=MESH)

    def rrs_start(d, _):
        rrs_copy(d).start()
        return 0

    lax.fori_loop(1, ROWS, rrs_start, 0)

    def lrs_wait(d, _):
        lrs_copy(d).wait_recv()
        return 0

    lax.fori_loop(1, COLS, lrs_wait, 0)
    f4t = dot_nt(tile4.T, f_ref[...]).astype(BF16)
    g4t = dot_nt(tile4.T, g_ref[...]).astype(BF16)
    zero = jnp.zeros((SL, 128), F32)
    for g in range(I // 4):
        sl = slice(g * 128, (g + 1) * 128)
        tot = lgt[mine, sl].astype(F32)
        for d in range(1, COLS):
            tot = tot + lgin[d, :, sl].astype(F32)
        rows4 = jnp.concatenate(
            [jnp.where(jnp.logical_and(ln128 >= 32 * a, ln128 < 32 * a + 32), tot, zero) for a in range(4)], axis=0)
        res = dot(rows4.astype(BF16), f4t)
        for a in range(4):
            for k in range(2):
                hg[k, pl.ds(4 * g + a, SL, stride=I), :] = res[a * SL:(a + 1) * SL, k * 128:(k + 1) * 128]

    def rrs_wait(d, _):
        rrs_copy(d).wait_recv()
        return 0

    lax.fori_loop(1, ROWS, rrs_wait, 0)
    for g in range(G8):
        tiles = []
        for m in range(3):
            sl = slice((3 * g + m) * 128, (3 * g + m + 1) * 128)
            tot = rgp[here, sl].astype(F32)
            for d in range(1, ROWS):
                tot = tot + rgin[d, :, sl].astype(F32)
            tiles.append(tot)
        tiles.append(unpack_fourth(*tiles))
        for k in range(2):
            even, odd = tiles[2 * k], tiles[2 * k + 1]
            rh[0, 2 * g + k] = jnp.where(ln16 < 64, even, roll(odd, 64)).astype(BF16)
            rh[1, 2 * g + k] = jnp.where(ln16 < 64, roll(even, 80), roll(odd, 16)).astype(BF16)
    for t in range(2):
        hop_start(rh.at[t], rhin.at[half], t, hop2_s, hop2_r.at[half])
    for t in range(2):
        hop_wait(rh.at[t], rhin.at[t], t, hop2_s, hop2_r.at[t])
    for qp in range(Q // 2):
        both = jnp.concatenate([rhin[0, qp], rhin[1, qp]], axis=0).astype(F32)
        tq[pl.ds(2 * qp, SL, stride=Q), :] = both
        tq[pl.ds(2 * qp + 1, SL, stride=Q), :] = roll(both, 64)
    iden_i = eye(I, 128)
    lni = lanes((I, 128))

    def finish(b, _):
        rows = 4 * I
        at = pl.multiple_of(b * rows, rows)
        tj = dot_nt(iden_i, tq[pl.ds(pl.multiple_of(b * 128, 128), 128), :].astype(BF16))
        parts = [jnp.where(jnp.logical_and(lni >= 32 * a, lni < 32 * a + 32), tj, 0.0) for a in range(4)]
        right = dot(jnp.concatenate(parts, axis=0).astype(BF16), g4t)
        left = jnp.concatenate([hg[0, pl.ds(at, rows), :], hg[1, pl.ds(at, rows), :]], axis=1)
        grad = (left + right) * scale
        xn = xhat[pl.ds(at, rows), :]
        m1 = jnp.mean(grad, axis=-1, keepdims=True)
        m2 = jnp.mean(grad * xn, axis=-1, keepdims=True)
        res = (grad - m1 - xn * m2) * rstd[pl.ds(at, rows), :]
        slope_ref[pl.ds(b * 4, 4)] = res.astype(BF16).reshape(4, I, CH)
        return 0

    lax.fori_loop(0, SL // 4, finish, 0)

    def drain_col(d, _):
        l_copy(d).wait_send()
        lrs_copy(d).wait_send()
        a2a_copy(d - 1).wait()
        return 0

    def drain_row(d, _):
        r_copy(d).wait_send()
        rrs_copy(d).wait_send()
        return 0

    lax.fori_loop(1, COLS, drain_col, 0)
    lax.fori_loop(1, ROWS, drain_row, 0)
    own_copy().wait()
    for t in range(2):
        hop_sent(rhop.at[:, pl.ds(SK * t, SK), :], rin.at[half], t, hop_s, hop_r.at[half])
        hop_sent(rh.at[t], rhin.at[half], t, hop2_s, hop2_r.at[half])


def on_device(*args):
    vmem = pl.BlockSpec(memory_space=pltpu.VMEM)
    dma = pltpu.SemaphoreType.DMA
    return pl.pallas_call(
        kernel,
        out_shape=(
            jax.ShapeDtypeStruct((IB, J * COLS, C), BF16),
            jax.ShapeDtypeStruct((I, J, C), BF16),
            jax.ShapeDtypeStruct((SL, I, CH), BF16),
        ),
        in_specs=[vmem] * 8,
        out_specs=(pl.BlockSpec(memory_space=pl.ANY), vmem, vmem),
        scratch_shapes=[
            pltpu.VMEM((SL * I, CH), F32),
            pltpu.VMEM((SL * I, 1), F32),
            pltpu.VMEM((SL * I, 128), F32),
            pltpu.VMEM((SL * Q, 128), F32),
            pltpu.VMEM((S, I * Q), BF16),
            pltpu.VMEM((I * Q, S), BF16),
            pltpu.VMEM((Q // 2, SL, 128), BF16),
            pltpu.VMEM((2, Q // 2, SK, 128), BF16),
            pltpu.VMEM((S, FULL), BF16),
            pltpu.VMEM((Q * Q, IB * JP), BF16),
            pltpu.VMEM((I * Q, FULL), BF16),
            pltpu.VMEM((I, J, C), BF16),
            pltpu.VMEM((Q * Q, C), F32),
            pltpu.VMEM((Q * Q, C), BF16),
            pltpu.VMEM((C, Q * Q), BF16),
            pltpu.VMEM((H, C), BF16),
            pltpu.VMEM((C, H), BF16),
            pltpu.VMEM((I * Q, S), BF16),
            pltpu.VMEM((S, I * Q), BF16),
            pltpu.VMEM((COLS, SL, I * Q), BF16),
            pltpu.VMEM((S, PK), BF16),
            pltpu.VMEM((ROWS, SK, PK), BF16),
            pltpu.VMEM((2, Q // 2, SK, 128), BF16),
            pltpu.VMEM((2, Q // 2, SK, 128), BF16),
            pltpu.VMEM((2, SL * I, 128), F32),
            dma((2,)), dma((2,)),
            dma((COLS,)), dma((COLS,)),
            dma((ROWS,)), dma((ROWS,)),
            dma((COLS,)), dma((COLS,)),
            dma((COLS,)), dma((COLS,)),
            dma((ROWS,)), dma((ROWS,)),
            dma((2,)), dma((2,)),
        ],
        compiler_params=pltpu.CompilerParams(
            collective_id=0, has_side_effects=True, vmem_limit_bytes=60 * 1024 * 1024),
        cost_estimate=pl.CostEstimate(flops=16_000_000_000, bytes_accessed=8_000_000, transcendentals=3_000_000),
    )(*args)


def solution(mesh):
    return jax.shard_map(
        on_device,
        mesh=mesh,
        in_specs=(P("col", "row", None), P("row", "col", None), P("row", "col", None), P(), P(), P(), P(), P()),
        out_specs=(P(("row", "col"), None, None), P("row", "col", None), P("col", "row", None)),
        check_vma=False,
    )
```

```python
import functools

import jax
import jax.numpy as jnp
from jax import lax
from jax.experimental import pallas as pl
from jax.experimental.pallas import tpu as pltpu
from jax.sharding import PartitionSpec as P

MESH = pl.DeviceIdType.MESH
EPS = 1e-05
F32 = jnp.float32
BF16 = jnp.bfloat16

ROWS, COLS = 16, 8
S, SL = 256, 32
I, J, JP = 48, 96, 128
Q = 32
C, H, CH = 128, 512, 256
SK = S // ROWS
G8 = Q // 4
PK = 3 * G8 * 128
FULL = Q * JP
IB = I // COLS
SLABS = [4 * (k // 3) + k % 3 for k in range(3 * G8)] + [4 * g + 3 for g in range(G8)]


def dot(a, b):
    return jnp.dot(a, b, preferred_element_type=F32)


def dot_nt(a, b):
    return lax.dot_general(a, b, (((1,), (1,)), ((), ())), preferred_element_type=F32)


def eye(n, m=None):
    m = n if m is None else m
    i = lax.broadcasted_iota(jnp.int32, (n, m), 0)
    j = lax.broadcasted_iota(jnp.int32, (n, m), 1)
    return jnp.where(i == j, 1.0, 0.0).astype(BF16)


def lanes(shape):
    return lax.broadcasted_iota(jnp.int32, shape, 1)


def roll(x, shift):
    return pltpu.roll(x, shift, 1)


def pack4(q0, q1, q2, q3):
    ln = lanes(q0.shape)
    return (
        jnp.where(ln < 96, q0, roll(q3, 96)),
        jnp.where(ln < 96, q1, roll(q3, 64)),
        jnp.where(ln < 96, q2, roll(q3, 32)),
    )


def unpack_fourth(t0, t1, t2):
    ln = lanes(t0.shape)
    return jnp.where(ln < 32, roll(t0, 32), jnp.where(ln < 64, roll(t1, 64), roll(t2, 96)))


def kernel(
    x_ref, pair_ref, loss_ref, f_ref, g_ref, w_ref, e_ref, s_ref,
    out_ref, grad_ref, slope_ref,
    xhat, rstd, proj, tq, lall, lt, rhop, rin, rm, xs, ogs, obuf,
    wf32, wf, wt, et, st, lgt, rgp, rh, rhin, hg, ct, lot, hgs, rmt, r_relay, r_main, l_relay, l_main, l_sib,
    hop_s, hop_r, ag_s, ag_r, sib_s, sib_r, a2a_s, a2a_r, rs_s, rs_r, hop2_s, hop2_r,
):
    r = lax.axis_index("row")
    c = lax.axis_index("col")
    half = lax.rem(r, 2)
    across = lax.div(r, 2)

    z, y = lax.div(r, 4), lax.rem(r, 4)
    x, core = lax.div(c, 2), lax.rem(c, 2)

    barrier = pltpu.get_barrier_semaphore()

    def at_row(z_, y_):
        return 4 * lax.rem(z_ + 4, 4) + lax.rem(y_ + 4, 4)

    def at_col(x_):
        return 2 * lax.rem(x_ + 4, 4) + core

    for row in (at_row(z - 1, y), at_row(z + 1, y), at_row(z, y - 1), at_row(z, y + 1)):
        pl.semaphore_signal(barrier, inc=1, device_id=(row, c), device_id_type=MESH)

    def greet_col(d, _):
        pl.semaphore_signal(barrier, inc=1, device_id=(r, lax.rem(c + d, COLS)), device_id_type=MESH)
        return 0

    lax.fori_loop(1, COLS, greet_col, 0)
    own = [jnp.logical_and(across == c, half == t) for t in range(2)]
    for t in range(2):
        @pl.when(jnp.logical_not(own[t]))
        def _():
            pl.semaphore_signal(barrier, inc=1, device_id=(2 * c + t, across), device_id_type=MESH)

    iden = eye(C)
    ln128 = lanes((SL, 128))
    tile4 = jnp.where(
        lax.rem(lax.broadcasted_iota(jnp.int32, (128, Q), 0), Q)
        == lax.broadcasted_iota(jnp.int32, (128, Q), 1), 1.0, 0.0).astype(BF16)
    f4t = dot(tile4, f_ref[...]).astype(BF16)
    g4t = dot(tile4, g_ref[...]).astype(BF16)
    tq[...] = jnp.zeros_like(tq)

    def project(b, _):
        rows = 4 * I
        at = pl.multiple_of(b * rows, rows)
        xr = x_ref[pl.ds(b * 4, 4)].reshape(rows, CH).astype(F32)
        center = xr - jnp.mean(xr, axis=-1, keepdims=True)
        inv = lax.rsqrt(jnp.mean(center * center, axis=-1, keepdims=True) + EPS)
        xn = center * inv
        xhat[pl.ds(at, rows), :] = xn
        rstd[pl.ds(at, rows), :] = inv
        xb = xn.astype(BF16)
        proj[pl.ds(at, rows), :] = dot_nt(xb, f4t)
        for k in range(4):
            to = pl.multiple_of((b * 4 + k) * Q, Q)
            tq[pl.ds(to, Q), 0:I] = dot_nt(g_ref[...], xb[k * I:(k + 1) * I])
        return 0

    lax.fori_loop(0, SL // 4, project, 0)

    mine = pl.ds(pl.multiple_of(c * SL, SL), SL)
    for qp in range(Q // 2):
        even = tq[pl.ds(2 * qp, SL, stride=Q), :]
        odd = tq[pl.ds(2 * qp + 1, SL, stride=Q), :]
        rhop[qp] = jnp.where(ln128 < 64, even, roll(odd, 64)).astype(BF16)
    for g in range(I // 4):
        parts = [proj[pl.ds(4 * g + a, SL, stride=I), :] for a in range(4)]
        tile = jnp.where(ln128 < 32, parts[0], jnp.where(ln128 < 64, parts[1],
                         jnp.where(ln128 < 96, parts[2], parts[3])))
        lall[mine, g * 128:(g + 1) * 128] = tile.astype(BF16)

    pl.semaphore_wait(barrier, 4 + COLS - 1 + 2 - (across == c).astype(jnp.int32))

    def hop_remote(src, dst, t, ss, rs):
        return pltpu.make_async_remote_copy(
            src_ref=src, dst_ref=dst, send_sem=ss.at[t], recv_sem=rs,
            device_id=(2 * c + t, across), device_id_type=MESH)

    def hop_start(src, dst, t, ss, rs):
        @pl.when(own[t])
        def _():
            pltpu.make_async_copy(src, dst, rs).start()

        @pl.when(jnp.logical_not(own[t]))
        def _():
            hop_remote(src, dst, t, ss, rs).start()

    def hop_wait(src, dst, t, ss, rs):
        @pl.when(own[t])
        def _():
            pltpu.make_async_copy(src, dst, rs).wait()

        @pl.when(jnp.logical_not(own[t]))
        def _():
            hop_remote(src, dst, t, ss, rs).wait_recv()

    def hop_sent(src, dst, t, ss, rs):
        @pl.when(jnp.logical_not(own[t]))
        def _():
            hop_remote(src, dst, t, ss, rs).wait_send()

    for t in range(2):
        hop_start(rhop.at[:, pl.ds(SK * t, SK), :], rin.at[half], t, hop_s, hop_r.at[half])

    wf32[...] = w_ref[...].astype(F32)
    for k, q in enumerate(SLABS):
        wf[k * Q:(k + 1) * Q, :] = wf32[pl.ds(q, Q, stride=Q), :].astype(BF16)
    wt[...] = dot_nt(iden, wf[...]).astype(BF16)
    st[...] = dot_nt(iden, s_ref[...]).astype(BF16)
    et[...] = dot_nt(eye(H), e_ref[...]).astype(BF16)
    pad = jnp.zeros((JP - J, C), BF16)

    def ahead(k, _):
        to = pl.ds(pl.multiple_of(k * 256, 256), 256)
        pr = jnp.concatenate([pair_ref[2 * k], pad, pair_ref[2 * k + 1], pad], axis=0)
        lo = jnp.concatenate([loss_ref[2 * k], pad, loss_ref[2 * k + 1], pad], axis=0)
        ct[:, to] = dot_nt(iden, pr).astype(BF16)
        lob = dot_nt(iden, lo).astype(BF16)
        lot[:, to] = lob
        hgs[:, to] = dot(s_ref[...], lob).astype(BF16)
        return 0

    lax.fori_loop(0, 12, ahead, 0)

    for t in range(2):
        hop_wait(rhop.at[:, pl.ds(SK * t, SK), :], rin.at[t], t, hop_s, hop_r.at[t])

    ln16 = lanes((SK, 128))
    here = pl.ds(pl.multiple_of(r * SK, SK), SK)
    for g in range(G8):
        tiles = []
        for k in range(2):
            a = rin[0, 2 * g + k].astype(F32)
            b = rin[1, 2 * g + k].astype(F32)
            tiles.append(jnp.where(ln16 < 48, a, roll(b, 48)))
            tiles.append(jnp.where(ln16 < 48, roll(a, 64), roll(b, 112)))
        for k, tile in enumerate(pack4(*tiles)):
            rm[here, (3 * g + k) * 128:(3 * g + k + 1) * 128] = tile.astype(BF16)

    def send(src, dst, ss, rs, to):
        return pltpu.make_async_remote_copy(
            src_ref=src, dst_ref=dst, send_sem=ss, recv_sem=rs, device_id=to, device_id_type=MESH)

    def gather_ring(sl, to, g):
        return [
            send(sl(0, 0, 2), sl(0, 0, 2), ag_s.at[g, 0], ag_r.at[g, 0], to(1)),
            send(sl(0, 0, 2), sl(0, 0, 2), ag_s.at[g, 1], ag_r.at[g, 1], to(-1)),
            send(sl(-1, 0, 1), sl(-1, 0, 1), ag_s.at[g, 2], ag_r.at[g, 2], to(1)),
            send(sl(1, 1, 1), sl(1, 1, 1), ag_s.at[g, 3], ag_r.at[g, 3], to(-1)),
        ]

    def scatter_ring(sl, relay, main, to, g):
        return [
            send(sl(2, 0, 1), relay.at[0], rs_s.at[g, 0], rs_r.at[g, 0], to(1)),
            send(sl(2, 1, 1), relay.at[1], rs_s.at[g, 1], rs_r.at[g, 1], to(-1)),
            send(sl(1, 0, 2), main.at[0], rs_s.at[g, 2], rs_r.at[g, 2], to(1)),
            send(sl(-1, 0, 2), main.at[1], rs_s.at[g, 3], rs_r.at[g, 3], to(-1)),
        ]

    def chunk(ref, side, along_z, w):
        def sl(off, first, count):
            row = at_row(z + off, y + w) if along_z else at_row(z + w, y + off)
            return ref.at[pl.ds(pl.multiple_of(row * SK, SK), SK), pl.ds(side * (PK // 2) + first * (PK // 4), count * (PK // 4))]
        return sl

    def along(along_z):
        return lambda d: (at_row(z + d, y), c) if along_z else (at_row(z, y + d), c)

    def l_chunk(ref):
        def sl(off, first, count):
            return ref.at[pl.ds(pl.multiple_of(at_col(x + off) * SL, SL), SL), pl.ds(first * (I * Q // 2), count * (I * Q // 2))]
        return sl

    def to_x(d):
        return (r, at_col(x + d))

    sibling = (r, c + 1 - 2 * core)
    STEPS = (0, -1, 1, 2)
    first = [gather_ring(chunk(rm, k, k == 1, 0), along(k == 1), 5 * k) for k in range(2)]
    second = [[gather_ring(chunk(rm, k, k == 0, w), along(k == 0), 5 * k + 1 + n)
               for n, w in enumerate(STEPS)] for k in range(2)]
    l_ring = gather_ring(l_chunk(lall), to_x, 10)
    l_sibs = [send(l_chunk(lall)(w, 0, 2), l_chunk(lall)(w, 0, 2), sib_s.at[n], sib_r.at[n], sibling)
              for n, w in enumerate(STEPS)]
    for k in range(2):
        first[k][0].start()
        first[k][1].start()
    for k in range(2):
        second[k][0][0].start()
        second[k][0][1].start()
    l_ring[0].start()
    l_ring[1].start()
    l_sibs[0].start()
    lax.fori_loop(12, 15, ahead, 0)
    for m in range(2):
        for k in range(2):
            first[k][m].wait_recv()
            first[k][2 + m].start()
            second[k][1 + m][0].start()
            second[k][1 + m][1].start()
    lax.fori_loop(15, 18, ahead, 0)
    for k in range(2):
        first[k][2].wait_recv()
        first[k][3].wait_recv()
        second[k][3][0].start()
        second[k][3][1].start()
    for m in range(2):
        l_ring[m].wait_recv()
        l_ring[2 + m].start()
        l_sibs[1 + m].start()
    for n in range(4):
        for m in range(2):
            for k in range(2):
                second[k][n][m].wait_recv()
                second[k][n][2 + m].start()
        if n < 2:
            lax.fori_loop(18 + 3 * n, 21 + 3 * n, ahead, 0)
    l_ring[2].wait_recv()
    l_ring[3].wait_recv()
    l_sibs[3].start()
    for n in range(4):
        l_sibs[n].wait_recv()
    e256 = eye(S)
    for k in range(I * Q // S):
        lt[k * S:(k + 1) * S, :] = dot_nt(e256, lall[:, k * S:(k + 1) * S]).astype(BF16)
    for n in range(4):
        for k in range(2):
            second[k][n][2].wait_recv()
            second[k][n][3].wait_recv()
    for g in range(G8):
        t0, t1, t2 = [rm[:, (3 * g + k) * 128:(3 * g + k + 1) * 128].astype(F32) for k in range(3)]
        rm[:, (3 * G8 + g) * 128:(3 * G8 + g + 1) * 128] = unpack_fourth(t0, t1, t2).astype(BF16)

    def a2a_copy(t):
        to = lax.rem(c + 1 + t, COLS)
        return pltpu.make_async_remote_copy(
            src_ref=obuf.at[pl.ds(to * IB, IB)], dst_ref=out_ref.at[:, pl.ds(pl.multiple_of(c * J, J), J), :],
            send_sem=a2a_s.at[t], recv_sem=a2a_r.at[t], device_id=(r, to), device_id_type=MESH)

    def own_copy():
        return pltpu.make_async_copy(
            obuf.at[pl.ds(c * IB, IB)], out_ref.at[:, pl.ds(pl.multiple_of(c * J, J), J), :],
            a2a_s.at[COLS - 1])

    scale = 1.0 / S

    def block(t, _):
        ib = lax.rem(c + 1 + t, COLS)
        ip = pl.ds(pl.multiple_of(ib * (IB * Q), IB * Q), IB * Q)
        ltb = lt[ip, :]
        for ch in range(8):
            d = dot(ltb, rm[:, ch * 512:(ch + 1) * 512]).astype(BF16)
            for k in range(4):
                slab = ch * 4 + k
                for i in range(IB):
                    xs[slab * Q:(slab + 1) * Q, i * JP:(i + 1) * JP] = d[i * Q:(i + 1) * Q, k * 128:(k + 1) * 128]
        for half_block in range(IB // 2):
            i0 = ib * IB + 2 * half_block
            ls = slice(half_block * 256, half_block * 256 + 256)
            upd = dot(wt[...], xs[:, ls]) * scale
            here_l = pl.ds(pl.multiple_of(i0 * JP, 2 * JP), 2 * JP)
            mid = (ct[:, here_l].astype(F32) + upd).astype(BF16).astype(F32)
            center = mid - jnp.mean(mid, axis=0, keepdims=True)
            inv = lax.rsqrt(jnp.mean(center * center, axis=0, keepdims=True) + EPS)
            xn = center * inv
            pre = dot(et[...], xn.astype(BF16))
            hgr = hgs[:, here_l].astype(F32)
            sg = 0.5 * jnp.tanh(0.5 * pre) + 0.5
            hid = pre * sg
            pgr = (hgr * (sg + hid * (1.0 - sg))).astype(BF16)
            outb = (mid + dot(st[...], hid.astype(BF16))).astype(BF16)
            hatg = dot(e_ref[...], pgr)
            m1 = jnp.mean(hatg, axis=0, keepdims=True)
            m2 = jnp.mean(hatg * xn, axis=0, keepdims=True)
            gb = (lot[:, here_l].astype(F32) + (hatg - m1 - xn * m2) * inv).astype(BF16)
            for i in range(2):
                sl = slice(i * JP, (i + 1) * JP)
                obuf[i0 + i] = dot_nt(iden[0:J], outb[:, sl]).astype(BF16)
                grad_ref[i0 + i] = dot_nt(iden[0:J], gb[:, sl]).astype(BF16)
            og = dot(wf[...], gb).astype(BF16)
            for i in range(2):
                to = pl.ds(pl.multiple_of((i0 + i) * Q, Q), Q)
                for k in range(Q):
                    ogs[to, k * 128:(k + 1) * 128] = og[k * Q:(k + 1) * Q, i * JP:(i + 1) * JP]

        @pl.when(t < COLS - 1)
        def _():
            a2a_copy(t).start()

        @pl.when(t == COLS - 1)
        def _():
            own_copy().start()

        return 0

    lax.fori_loop(0, COLS, block, 0)

    big = [[scatter_ring(chunk(rgp, k, k == 0, w), r_relay.at[k, n], r_main.at[k, n], along(k == 0), 5 * k + n)
            for n, w in enumerate(STEPS)] for k in range(2)]
    small = [scatter_ring(chunk(rgp, k, k == 1, 0), r_relay.at[k, 4], r_main.at[k, 4], along(k == 1), 5 * k + 4)
             for k in range(2)]
    for g in range(0, G8, 2):
        a = dot(lall[...], ogs[:, 3 * g * 128:(3 * g + 6) * 128])
        b = dot(lall[...], ogs[:, (3 * G8 + g) * 128:(3 * G8 + g + 2) * 128])
        for k in range(2):
            tiles = pack4(*[a[:, (3 * k + m) * 128:(3 * k + m + 1) * 128] for m in range(3)],
                          b[:, k * 128:(k + 1) * 128])
            for m in range(3):
                at = (3 * (g + k) + m) * 128
                rgp[:, at:at + 128] = tiles[m].astype(BF16)
        if g % 4 == 2:
            for n in range(4):
                big[g // 4][n][0].start()
                big[g // 4][n][1].start()

    def add(dst, *srcs):
        tot = dst[...].astype(F32)
        for src in srcs:
            tot = tot + src[...].astype(F32)
        dst[...] = tot.astype(BF16)

    def left_grad(k):
        part = dot(ogs[k * S:(k + 1) * S, :], rmt[...]).astype(BF16)
        lgt[:, k * S:(k + 1) * S] = dot_nt(e256, part).astype(BF16)

    def relayed(ring, sl, relay):
        ring[0].wait_recv()
        add(sl(1, 0, 1), relay.at[0])
        ring[2].start()
        ring[1].wait_recv()
        add(sl(-1, 1, 1), relay.at[1])
        ring[3].start()

    for ch in range(FULL // S):
        rmt[ch * S:(ch + 1) * S, :] = dot_nt(e256, rm[:, ch * S:(ch + 1) * S]).astype(BF16)
    left_grad(0)
    for n, w in enumerate(STEPS):
        for k in range(2):
            relayed(big[k][n], chunk(rgp, k, k == 0, w), r_relay.at[k, n])
    for k in range(1, I * Q // S):
        left_grad(k)
    l_swap = [send(lgt.at[pl.ds(pl.multiple_of((2 * n + 1 - core) * SL, SL), SL)], l_sib.at[n],
                   sib_s.at[4 + n], sib_r.at[4 + n], sibling) for n in range(4)]
    for n in range(4):
        l_swap[n].start()
    for n, w in reversed(list(enumerate(STEPS))):
        for k in range(2):
            big[k][n][2].wait_recv()
            big[k][n][3].wait_recv()
            add(chunk(rgp, k, k == 0, w)(0, 0, 2), r_main.at[k, n, 0], r_main.at[k, n, 1])
    for k in range(2):
        small[k][0].start()
        small[k][1].start()
    for n in range(4):
        l_swap[n].wait_recv()
        add(lgt.at[pl.ds(pl.multiple_of((2 * n + core) * SL, SL), SL)], l_sib.at[n])
    l_back = scatter_ring(l_chunk(lgt), l_relay, l_main, to_x, 10)
    l_back[0].start()
    l_back[1].start()
    for k in range(2):
        relayed(small[k], chunk(rgp, k, k == 1, 0), r_relay.at[k, 4])
    relayed(l_back, l_chunk(lgt), l_relay)
    for k in range(2):
        small[k][2].wait_recv()
        small[k][3].wait_recv()
    for g in range(G8):
        tiles = []
        for m in range(3):
            at = (3 * g + m) * 128
            k, sl = at // (PK // 2), slice(at % (PK // 2), at % (PK // 2) + 128)
            tiles.append(rgp[here, at:at + 128].astype(F32) + r_main[k, 4, 0, :, sl].astype(F32)
                         + r_main[k, 4, 1, :, sl].astype(F32))
        tiles.append(unpack_fourth(*tiles))
        for k in range(2):
            even, odd = tiles[2 * k], tiles[2 * k + 1]
            rh[0, 2 * g + k] = jnp.where(ln16 < 64, even, roll(odd, 64)).astype(BF16)
            rh[1, 2 * g + k] = jnp.where(ln16 < 64, roll(even, 80), roll(odd, 16)).astype(BF16)
    for t in range(2):
        hop_start(rh.at[t], rhin.at[half], t, hop2_s, hop2_r.at[half])
    l_back[2].wait_recv()
    l_back[3].wait_recv()
    zero = jnp.zeros((SL, 128), F32)
    for g in range(I // 4):
        sl = slice(g * 128, (g + 1) * 128)
        tot = lgt[mine, sl].astype(F32) + l_main[0, :, sl].astype(F32) + l_main[1, :, sl].astype(F32)
        rows4 = jnp.concatenate(
            [jnp.where(jnp.logical_and(ln128 >= 32 * a, ln128 < 32 * a + 32), tot, zero) for a in range(4)], axis=0)
        res = dot(rows4.astype(BF16), f4t)
        for a in range(4):
            for k in range(2):
                hg[k, pl.ds(4 * g + a, SL, stride=I), :] = res[a * SL:(a + 1) * SL, k * 128:(k + 1) * 128]
    for t in range(2):
        hop_wait(rh.at[t], rhin.at[t], t, hop2_s, hop2_r.at[t])
    for qp in range(Q // 2):
        both = jnp.concatenate([rhin[0, qp], rhin[1, qp]], axis=0).astype(F32)
        tq[pl.ds(2 * qp, SL, stride=Q), :] = both
        tq[pl.ds(2 * qp + 1, SL, stride=Q), :] = roll(both, 64)
    iden_i = eye(I, 128)
    lni = lanes((I, 128))

    def finish(b, _):
        rows = 4 * I
        at = pl.multiple_of(b * rows, rows)
        tj = dot_nt(iden_i, tq[pl.ds(pl.multiple_of(b * 128, 128), 128), :].astype(BF16))
        parts = [jnp.where(jnp.logical_and(lni >= 32 * a, lni < 32 * a + 32), tj, 0.0) for a in range(4)]
        right = dot(jnp.concatenate(parts, axis=0).astype(BF16), g4t)
        left = jnp.concatenate([hg[0, pl.ds(at, rows), :], hg[1, pl.ds(at, rows), :]], axis=1)
        grad = (left + right) * scale
        xn = xhat[pl.ds(at, rows), :]
        m1 = jnp.mean(grad, axis=-1, keepdims=True)
        m2 = jnp.mean(grad * xn, axis=-1, keepdims=True)
        res = (grad - m1 - xn * m2) * rstd[pl.ds(at, rows), :]
        slope_ref[pl.ds(b * 4, 4)] = res.astype(BF16).reshape(4, I, CH)
        return 0

    lax.fori_loop(0, SL // 4, finish, 0)

    def drain(t, _):
        a2a_copy(t).wait()
        return 0

    lax.fori_loop(0, COLS - 1, drain, 0)
    for ring in first + second[0] + second[1] + big[0] + big[1] + small + [l_ring, l_back, l_sibs, l_swap]:
        for copy in ring:
            copy.wait_send()
    own_copy().wait()
    for t in range(2):
        hop_sent(rhop.at[:, pl.ds(SK * t, SK), :], rin.at[half], t, hop_s, hop_r.at[half])
        hop_sent(rh.at[t], rhin.at[half], t, hop2_s, hop2_r.at[half])


def on_device(profile, pair, loss, former, latter, mixing, expand, shrink):
    vmem = pl.BlockSpec(memory_space=pltpu.VMEM)
    dma = pltpu.SemaphoreType.DMA
    return pl.pallas_call(
        kernel,
        out_shape=(
            jax.ShapeDtypeStruct((IB, J * COLS, C), BF16),
            jax.ShapeDtypeStruct((I, J, C), BF16),
            jax.ShapeDtypeStruct((SL, I, CH), BF16),
        ),
        in_specs=[vmem] * 8,
        out_specs=(pl.BlockSpec(memory_space=pl.ANY), vmem, vmem),
        scratch_shapes=[
            pltpu.VMEM((SL * I, CH), F32),
            pltpu.VMEM((SL * I, 1), F32),
            pltpu.VMEM((SL * I, 128), F32),
            pltpu.VMEM((SL * Q, 128), F32),
            pltpu.VMEM((S, I * Q), BF16),
            pltpu.VMEM((I * Q, S), BF16),
            pltpu.VMEM((Q // 2, SL, 128), BF16),
            pltpu.VMEM((2, Q // 2, SK, 128), BF16),
            pltpu.VMEM((S, FULL), BF16),
            pltpu.VMEM((Q * Q, IB * JP), BF16),
            pltpu.VMEM((I * Q, FULL), BF16),
            pltpu.VMEM((I, J, C), BF16),
            pltpu.VMEM((Q * Q, C), F32),
            pltpu.VMEM((Q * Q, C), BF16),
            pltpu.VMEM((C, Q * Q), BF16),
            pltpu.VMEM((H, C), BF16),
            pltpu.VMEM((C, H), BF16),
            pltpu.VMEM((S, I * Q), BF16),
            pltpu.VMEM((S, PK), BF16),
            pltpu.VMEM((2, Q // 2, SK, 128), BF16),
            pltpu.VMEM((2, Q // 2, SK, 128), BF16),
            pltpu.VMEM((2, SL * I, 128), F32),
            pltpu.VMEM((C, I * JP), BF16),
            pltpu.VMEM((C, I * JP), BF16),
            pltpu.VMEM((H, I * JP), BF16),
            pltpu.VMEM((FULL, S), BF16),
            pltpu.VMEM((2, 5, 2, SK, PK // 4), BF16),
            pltpu.VMEM((2, 5, 2, SK, PK // 2), BF16),
            pltpu.VMEM((2, SL, I * Q // 2), BF16),
            pltpu.VMEM((2, SL, I * Q), BF16),
            pltpu.VMEM((4, SL, I * Q), BF16),
            dma((2,)), dma((2,)),
            dma((11, 4)), dma((11, 4)),
            dma((8,)), dma((8,)),
            dma((COLS,)), dma((COLS,)),
            dma((11, 4)), dma((11, 4)),
            dma((2,)), dma((2,)),
        ],
        compiler_params=pltpu.CompilerParams(
            collective_id=0, has_side_effects=True, vmem_limit_bytes=60 * 1024 * 1024),
        cost_estimate=pl.CostEstimate(flops=16_000_000_000, bytes_accessed=8_000_000, transcendentals=3_000_000),
    )(profile, pair, loss, former.T, latter.T, mixing, expand, shrink)


def solution(mesh):
    return jax.shard_map(
        on_device,
        mesh=mesh,
        in_specs=(P("col", "row", None), P("row", "col", None), P("row", "col", None), P(), P(), P(), P(), P()),
        out_specs=(P(("row", "col"), None, None), P("row", "col", None), P("col", "row", None)),
        check_vma=False,
    )
```

```python
import functools

import jax
import jax.numpy as jnp
from jax import lax
from jax.experimental import pallas as pl
from jax.experimental.pallas import tpu as pltpu
from jax.sharding import PartitionSpec as P

MESH = pl.DeviceIdType.MESH
EPS = 1e-05
F32 = jnp.float32
BF16 = jnp.bfloat16

ROWS, COLS = 16, 8
S, SL = 256, 32
I, J, JP = 48, 96, 128
Q = 32
C, H, CH = 128, 512, 256
SK = S // ROWS
G8 = Q // 4
PK = 3 * G8 * 128
FULL = Q * JP
IB = I // COLS
SLABS = [4 * (k // 3) + k % 3 for k in range(3 * G8)] + [4 * g + 3 for g in range(G8)]


def dot(a, b):
    return jnp.dot(a, b, preferred_element_type=F32)


def dot_nt(a, b):
    return lax.dot_general(a, b, (((1,), (1,)), ((), ())), preferred_element_type=F32)


def eye(n, m=None):
    m = n if m is None else m
    i = lax.broadcasted_iota(jnp.int32, (n, m), 0)
    j = lax.broadcasted_iota(jnp.int32, (n, m), 1)
    return jnp.where(i == j, 1.0, 0.0).astype(BF16)


def lanes(shape):
    return lax.broadcasted_iota(jnp.int32, shape, 1)


def roll(x, shift):
    return pltpu.roll(x, shift, 1)


def pack4(q0, q1, q2, q3):
    ln = lanes(q0.shape)
    return (
        jnp.where(ln < 96, q0, roll(q3, 96)),
        jnp.where(ln < 96, q1, roll(q3, 64)),
        jnp.where(ln < 96, q2, roll(q3, 32)),
    )


def squeeze(t0, t1, t2, t3):
    inner = lax.rem(lanes(t0.shape), 64)
    return [jnp.where(inner < 48, t, roll(t3, 48 - 16 * k)) for k, t in enumerate((t0, t1, t2))]


def restore(t0, t1, t2):
    inner = lax.rem(lanes(t0.shape), 64)
    return [t0, t1, t2, jnp.where(inner < 16, roll(t0, 80), jnp.where(inner < 32, roll(t1, 96), roll(t2, 112)))]


def unpack_fourth(t0, t1, t2):
    ln = lanes(t0.shape)
    return jnp.where(ln < 32, roll(t0, 32), jnp.where(ln < 64, roll(t1, 64), roll(t2, 96)))


def kernel(
    x_ref, pair_ref, loss_ref, f_ref, g_ref, w_ref, e_ref, s_ref,
    out_ref, grad_ref, slope_ref,
    xhat, rstd, proj, tq, lall, lt, rhop, rin, rm, xs, ogs, obuf,
    wf32, wf, wt, et, st, lgt, rgp, rh, rhin, hg, ct, lot, hgs, r_relay, r_main, r_small, l_relay, l_main, l_sib,
    hop_s, hop_r, ag_s, ag_r, sib_s, sib_r, a2a_s, a2a_r, rs_s, rs_r, hop2_s, hop2_r,
):
    r = lax.axis_index("row")
    c = lax.axis_index("col")
    half = lax.rem(r, 2)
    across = lax.div(r, 2)

    z, y = lax.div(r, 4), lax.rem(r, 4)
    x, core = lax.div(c, 2), lax.rem(c, 2)

    barrier = pltpu.get_barrier_semaphore()

    def at_row(z_, y_):
        return 4 * lax.rem(z_ + 4, 4) + lax.rem(y_ + 4, 4)

    def at_col(x_):
        return 2 * lax.rem(x_ + 4, 4) + core

    for row in (at_row(z - 1, y), at_row(z + 1, y), at_row(z + 2, y), at_row(z, y - 1), at_row(z, y + 1), at_row(z, y + 2)):
        pl.semaphore_signal(barrier, inc=1, device_id=(row, c), device_id_type=MESH)

    def greet_col(d, _):
        pl.semaphore_signal(barrier, inc=1, device_id=(r, lax.rem(c + d, COLS)), device_id_type=MESH)
        return 0

    lax.fori_loop(1, COLS, greet_col, 0)
    own = [jnp.logical_and(across == c, half == t) for t in range(2)]
    for t in range(2):
        @pl.when(jnp.logical_not(own[t]))
        def _():
            pl.semaphore_signal(barrier, inc=1, device_id=(2 * c + t, across), device_id_type=MESH)

    iden = eye(C)
    ln128 = lanes((SL, 128))
    tile4 = jnp.where(
        lax.rem(lax.broadcasted_iota(jnp.int32, (128, Q), 0), Q)
        == lax.broadcasted_iota(jnp.int32, (128, Q), 1), 1.0, 0.0).astype(BF16)
    f4t = dot(tile4, f_ref[...]).astype(BF16)
    g4t = dot(tile4, g_ref[...]).astype(BF16)
    tq[...] = jnp.zeros_like(tq)

    def project(b, _):
        rows = 4 * I
        at = pl.multiple_of(b * rows, rows)
        xr = x_ref[pl.ds(b * 4, 4)].reshape(rows, CH).astype(F32)
        center = xr - jnp.mean(xr, axis=-1, keepdims=True)
        inv = lax.rsqrt(jnp.mean(center * center, axis=-1, keepdims=True) + EPS)
        xn = center * inv
        xhat[pl.ds(at, rows), :] = xn
        rstd[pl.ds(at, rows), :] = inv
        xb = xn.astype(BF16)
        proj[pl.ds(at, rows), :] = dot_nt(xb, f4t)
        for k in range(4):
            to = pl.multiple_of((b * 4 + k) * Q, Q)
            tq[pl.ds(to, Q), 0:I] = dot_nt(g_ref[...], xb[k * I:(k + 1) * I])
        return 0

    lax.fori_loop(0, SL // 4, project, 0)

    mine = pl.ds(pl.multiple_of(c * SL, SL), SL)
    for m in range(4):
        pairs = []
        for qp in range(4 * m, 4 * m + 4):
            even = tq[pl.ds(2 * qp, SL, stride=Q), :]
            odd = tq[pl.ds(2 * qp + 1, SL, stride=Q), :]
            pairs.append(jnp.where(ln128 < 64, even, roll(odd, 64)))
        for k, tile in enumerate(squeeze(*pairs)):
            rhop[3 * m + k] = tile.astype(BF16)
    for g in range(I // 4):
        parts = [proj[pl.ds(4 * g + a, SL, stride=I), :] for a in range(4)]
        tile = jnp.where(ln128 < 32, parts[0], jnp.where(ln128 < 64, parts[1],
                         jnp.where(ln128 < 96, parts[2], parts[3])))
        lall[mine, g * 128:(g + 1) * 128] = tile.astype(BF16)

    pl.semaphore_wait(barrier, 6 + COLS - 1 + 2 - (across == c).astype(jnp.int32))

    def hop_remote(src, dst, t, ss, rs):
        return pltpu.make_async_remote_copy(
            src_ref=src, dst_ref=dst, send_sem=ss.at[t], recv_sem=rs,
            device_id=(2 * c + t, across), device_id_type=MESH)

    def hop_start(src, dst, t, ss, rs):
        @pl.when(own[t])
        def _():
            pltpu.make_async_copy(src, dst, rs).start()

        @pl.when(jnp.logical_not(own[t]))
        def _():
            hop_remote(src, dst, t, ss, rs).start()

    def hop_wait(src, dst, t, ss, rs):
        @pl.when(own[t])
        def _():
            pltpu.make_async_copy(src, dst, rs).wait()

        @pl.when(jnp.logical_not(own[t]))
        def _():
            hop_remote(src, dst, t, ss, rs).wait_recv()

    def hop_sent(src, dst, t, ss, rs):
        @pl.when(jnp.logical_not(own[t]))
        def _():
            hop_remote(src, dst, t, ss, rs).wait_send()

    for t in range(2):
        hop_start(rhop.at[:, pl.ds(SK * t, SK), :], rin.at[half], t, hop_s, hop_r.at[half])

    wf32[...] = w_ref[...].astype(F32)
    for k, q in enumerate(SLABS):
        wf[k * Q:(k + 1) * Q, :] = wf32[pl.ds(q, Q, stride=Q), :].astype(BF16)
    wt[...] = dot_nt(iden, wf[...]).astype(BF16)
    st[...] = dot_nt(iden, s_ref[...]).astype(BF16)
    et[...] = dot_nt(eye(H), e_ref[...]).astype(BF16)
    pad = jnp.zeros((JP - J, C), BF16)

    def ahead(k, _):
        to = pl.ds(pl.multiple_of(k * 256, 256), 256)
        pr = jnp.concatenate([pair_ref[2 * k], pad, pair_ref[2 * k + 1], pad], axis=0)
        lo = jnp.concatenate([loss_ref[2 * k], pad, loss_ref[2 * k + 1], pad], axis=0)
        ct[:, to] = pr.T
        lob = lo.T
        lot[:, to] = lob
        hgs[:, to] = dot(s_ref[...], lob).astype(BF16)
        return 0

    lax.fori_loop(0, 12, ahead, 0, unroll=6)

    for t in range(2):
        hop_wait(rhop.at[:, pl.ds(SK * t, SK), :], rin.at[t], t, hop_s, hop_r.at[t])

    ln16 = lanes((SK, 128))
    here = pl.ds(pl.multiple_of(r * SK, SK), SK)
    loose = [sum((restore(*[rin[n, 3 * m + k].astype(F32) for k in range(3)]) for m in range(4)), []) for n in range(2)]
    for g in range(G8):
        tiles = []
        for k in range(2):
            a, b = loose[0][2 * g + k], loose[1][2 * g + k]
            tiles.append(jnp.where(ln16 < 48, a, roll(b, 48)))
            tiles.append(jnp.where(ln16 < 48, roll(a, 64), roll(b, 112)))
        for k, tile in enumerate(pack4(*tiles)):
            rm[here, (3 * g + k) * 128:(3 * g + k + 1) * 128] = tile.astype(BF16)

    def send(src, dst, ss, rs, to):
        return pltpu.make_async_remote_copy(
            src_ref=src, dst_ref=dst, send_sem=ss, recv_sem=rs, device_id=to, device_id_type=MESH)

    def gather_ring(sl, to, g):
        return [
            send(sl(0, 0, 2), sl(0, 0, 2), ag_s.at[g, 0], ag_r.at[g, 0], to(1)),
            send(sl(0, 0, 2), sl(0, 0, 2), ag_s.at[g, 1], ag_r.at[g, 1], to(-1)),
            send(sl(-1, 0, 1), sl(-1, 0, 1), ag_s.at[g, 2], ag_r.at[g, 2], to(1)),
            send(sl(1, 1, 1), sl(1, 1, 1), ag_s.at[g, 3], ag_r.at[g, 3], to(-1)),
        ]

    def gather_direct(sl, to, g):
        return [send(sl(0, 0, 2), sl(0, 0, 2), ag_s.at[g, k], ag_r.at[g, k], to(d)) for k, d in enumerate((1, -1, 2))]

    def scatter_direct(sl, into, to, g):
        return [send(sl(d, 0, 2), into.at[k], rs_s.at[g, k], rs_r.at[g, k], to(d)) for k, d in enumerate((1, -1, 2))]

    def scatter_ring(sl, relay, main, to, g):
        return [
            send(sl(2, 0, 1), relay.at[0], rs_s.at[g, 0], rs_r.at[g, 0], to(1)),
            send(sl(2, 1, 1), relay.at[1], rs_s.at[g, 1], rs_r.at[g, 1], to(-1)),
            send(sl(1, 0, 2), main.at[0], rs_s.at[g, 2], rs_r.at[g, 2], to(1)),
            send(sl(-1, 0, 2), main.at[1], rs_s.at[g, 3], rs_r.at[g, 3], to(-1)),
        ]

    def chunk(ref, side, along_z, w):
        def sl(off, first, count):
            row = at_row(z + off, y + w) if along_z else at_row(z + w, y + off)
            return ref.at[pl.ds(pl.multiple_of(row * SK, SK), SK), pl.ds(side * (PK // 2) + first * (PK // 4), count * (PK // 4))]
        return sl

    def along(along_z):
        return lambda d: (at_row(z + d, y), c) if along_z else (at_row(z, y + d), c)

    def l_chunk(ref):
        def sl(off, first, count):
            return ref.at[pl.ds(pl.multiple_of(at_col(x + off) * SL, SL), SL), pl.ds(first * (I * Q // 2), count * (I * Q // 2))]
        return sl

    def to_x(d):
        return (r, at_col(x + d))

    sibling = (r, c + 1 - 2 * core)
    STEPS = (0, -1, 1, 2)
    first = [gather_direct(chunk(rm, k, k == 1, 0), along(k == 1), 5 * k) for k in range(2)]
    second = [[gather_ring(chunk(rm, k, k == 0, w), along(k == 0), 5 * k + 1 + n)
               for n, w in enumerate(STEPS)] for k in range(2)]
    l_ring = gather_ring(l_chunk(lall), to_x, 10)
    l_sibs = [send(l_chunk(lall)(w, 0, 2), l_chunk(lall)(w, 0, 2), sib_s.at[n], sib_r.at[n], sibling)
              for n, w in enumerate(STEPS)]
    for k in range(2):
        for copy in first[k]:
            copy.start()
    for k in range(2):
        second[k][0][0].start()
        second[k][0][1].start()
    l_ring[0].start()
    l_ring[1].start()
    l_sibs[0].start()
    lax.fori_loop(12, 15, ahead, 0, unroll=3)
    for m in range(2):
        for k in range(2):
            first[k][m].wait_recv()
            second[k][1 + m][0].start()
            second[k][1 + m][1].start()
    lax.fori_loop(15, 18, ahead, 0, unroll=3)
    for k in range(2):
        first[k][2].wait_recv()
        second[k][3][0].start()
        second[k][3][1].start()
    for m in range(2):
        l_ring[m].wait_recv()
        l_ring[2 + m].start()
        l_sibs[1 + m].start()
    for n in range(4):
        for m in range(2):
            for k in range(2):
                second[k][n][m].wait_recv()
                second[k][n][2 + m].start()
        if n < 2:
            lax.fori_loop(18 + 3 * n, 21 + 3 * n, ahead, 0, unroll=3)
    l_ring[2].wait_recv()
    l_ring[3].wait_recv()
    l_sibs[3].start()
    for n in range(4):
        l_sibs[n].wait_recv()
    for k in range(I * Q // S):
        lt[k * S:(k + 1) * S, :] = lall[:, k * S:(k + 1) * S].T
    for n in range(4):
        for k in range(2):
            second[k][n][2].wait_recv()
            second[k][n][3].wait_recv()
    for g in range(G8):
        t0, t1, t2 = [rm[:, (3 * g + k) * 128:(3 * g + k + 1) * 128].astype(F32) for k in range(3)]
        rm[:, (3 * G8 + g) * 128:(3 * G8 + g + 1) * 128] = unpack_fourth(t0, t1, t2).astype(BF16)

    def a2a_copy(t):
        to = lax.rem(c + 1 + t, COLS)
        return pltpu.make_async_remote_copy(
            src_ref=obuf.at[pl.ds(to * IB, IB)], dst_ref=out_ref.at[:, pl.ds(pl.multiple_of(c * J, J), J), :],
            send_sem=a2a_s.at[t], recv_sem=a2a_r.at[t], device_id=(r, to), device_id_type=MESH)

    def own_copy():
        return pltpu.make_async_copy(
            obuf.at[pl.ds(c * IB, IB)], out_ref.at[:, pl.ds(pl.multiple_of(c * J, J), J), :],
            a2a_s.at[COLS - 1])

    scale = 1.0 / S

    def mix(b, _):
        for k in range(2):
            at = pl.multiple_of((2 * b + k) * 256, 256)
            ltb = lt[pl.ds(at, 256), :]
            for ch in range(8):
                d = dot(ltb, rm[:, ch * 512:(ch + 1) * 512]).astype(BF16)
                for m in range(4):
                    slab = ch * 4 + m
                    for i in range(8):
                        xs[k, slab * Q:(slab + 1) * Q, i * JP:(i + 1) * JP] = d[i * Q:(i + 1) * Q, m * 128:(m + 1) * 128]
        for k in range(2):
            to = pl.ds(pl.multiple_of((2 * b + k) * 1024, 1024), 1024)
            ct[:, to] = (ct[:, to].astype(F32) + dot(wt[...], xs[k]) * scale).astype(BF16)
        return 0

    lax.fori_loop(0, I // 16, mix, 0)

    def block(t, _):
        ib = lax.rem(c + 1 + t, COLS)
        for half_block in range(IB // 2):
            i0 = ib * IB + 2 * half_block
            here_l = pl.ds(pl.multiple_of(i0 * JP, 2 * JP), 2 * JP)
            mid = ct[:, here_l].astype(F32)
            center = mid - jnp.mean(mid, axis=0, keepdims=True)
            inv = lax.rsqrt(jnp.mean(center * center, axis=0, keepdims=True) + EPS)
            xn = center * inv
            pre = dot(et[...], xn.astype(BF16))
            hgr = hgs[:, here_l].astype(F32)
            sg = 0.5 * jnp.tanh(0.5 * pre) + 0.5
            hid = pre * sg
            pgr = (hgr * (sg + hid * (1.0 - sg))).astype(BF16)
            outb = (mid + dot(st[...], hid.astype(BF16))).astype(BF16)
            hatg = dot(e_ref[...], pgr)
            m1 = jnp.mean(hatg, axis=0, keepdims=True)
            m2 = jnp.mean(hatg * xn, axis=0, keepdims=True)
            gb = (lot[:, here_l].astype(F32) + (hatg - m1 - xn * m2) * inv).astype(BF16)
            for i in range(2):
                sl = slice(i * JP, (i + 1) * JP)
                obuf[i0 + i] = outb[:, sl].T[0:J]
                grad_ref[i0 + i] = gb[:, sl].T[0:J]
            og = dot(wf[...], gb).astype(BF16)
            for i in range(2):
                to = pl.ds(pl.multiple_of((i0 + i) * Q, Q), Q)
                for k in range(Q):
                    ogs[to, k * 128:(k + 1) * 128] = og[k * Q:(k + 1) * Q, i * JP:(i + 1) * JP]

        @pl.when(t < COLS - 1)
        def _():
            a2a_copy(t).start()

        @pl.when(t == COLS - 1)
        def _():
            own_copy().start()

        return 0

    lax.fori_loop(0, COLS, block, 0)

    big = [[scatter_ring(chunk(rgp, k, k == 0, w), r_relay.at[k, n], r_main.at[k, n], along(k == 0), 5 * k + n)
            for n, w in enumerate(STEPS)] for k in range(2)]
    small = [scatter_direct(chunk(rgp, k, k == 1, 0), r_small.at[k], along(k == 1), 5 * k + 4)
             for k in range(2)]
    for g in range(0, G8, 2):
        a = dot(lall[...], ogs[:, 3 * g * 128:(3 * g + 6) * 128])
        b = dot(lall[...], ogs[:, (3 * G8 + g) * 128:(3 * G8 + g + 2) * 128])
        for k in range(2):
            tiles = pack4(*[a[:, (3 * k + m) * 128:(3 * k + m + 1) * 128] for m in range(3)],
                          b[:, k * 128:(k + 1) * 128])
            for m in range(3):
                at = (3 * (g + k) + m) * 128
                rgp[:, at:at + 128] = tiles[m].astype(BF16)
        if g % 4 == 2:
            for n in range(4):
                big[g // 4][n][0].start()
                big[g // 4][n][1].start()

    def add(dst, *srcs):
        tot = dst[...].astype(F32)
        for src in srcs:
            tot = tot + src[...].astype(F32)
        dst[...] = tot.astype(BF16)

    def left_grad(k):
        lgt[:, k * S:(k + 1) * S] = dot_nt(rm[...], ogs[k * S:(k + 1) * S, :]).astype(BF16)

    def relayed(ring, sl, relay):
        ring[0].wait_recv()
        add(sl(1, 0, 1), relay.at[0])
        ring[2].start()
        ring[1].wait_recv()
        add(sl(-1, 1, 1), relay.at[1])
        ring[3].start()

    left_grad(0)
    for n, w in enumerate(STEPS):
        for k in range(2):
            relayed(big[k][n], chunk(rgp, k, k == 0, w), r_relay.at[k, n])
    for k in range(1, I * Q // S):
        left_grad(k)
    l_swap = [send(lgt.at[pl.ds(pl.multiple_of((2 * n + 1 - core) * SL, SL), SL)], l_sib.at[n],
                   sib_s.at[4 + n], sib_r.at[4 + n], sibling) for n in range(4)]
    for n in range(4):
        l_swap[n].start()
    for n, w in reversed(list(enumerate(STEPS))):
        for k in range(2):
            big[k][n][2].wait_recv()
            big[k][n][3].wait_recv()
            add(chunk(rgp, k, k == 0, w)(0, 0, 2), r_main.at[k, n, 0], r_main.at[k, n, 1])
    for k in range(2):
        for copy in small[k]:
            copy.start()
    for n in range(4):
        l_swap[n].wait_recv()
        add(lgt.at[pl.ds(pl.multiple_of((2 * n + core) * SL, SL), SL)], l_sib.at[n])
    l_back = scatter_ring(l_chunk(lgt), l_relay, l_main, to_x, 10)
    l_back[0].start()
    l_back[1].start()
    relayed(l_back, l_chunk(lgt), l_relay)
    for k in range(2):
        for copy in small[k]:
            copy.wait_recv()
    loose = [[], []]
    for g in range(G8):
        tiles = []
        for m in range(3):
            at = (3 * g + m) * 128
            k, sl = at // (PK // 2), slice(at % (PK // 2), at % (PK // 2) + 128)
            tot = rgp[here, at:at + 128].astype(F32)
            for n in range(3):
                tot = tot + r_small[k, n, :, sl].astype(F32)
            tiles.append(tot)
        tiles.append(unpack_fourth(*tiles))
        for k in range(2):
            even, odd = tiles[2 * k], tiles[2 * k + 1]
            loose[0].append(jnp.where(ln16 < 64, even, roll(odd, 64)))
            loose[1].append(jnp.where(ln16 < 64, roll(even, 80), roll(odd, 16)))
    for n in range(2):
        for m in range(4):
            for k, tile in enumerate(squeeze(*loose[n][4 * m:4 * m + 4])):
                rh[n, 3 * m + k] = tile.astype(BF16)
    for t in range(2):
        hop_start(rh.at[t], rhin.at[half], t, hop2_s, hop2_r.at[half])
    l_back[2].wait_recv()
    l_back[3].wait_recv()
    zero = jnp.zeros((SL, 128), F32)
    for g in range(I // 4):
        sl = slice(g * 128, (g + 1) * 128)
        tot = lgt[mine, sl].astype(F32) + l_main[0, :, sl].astype(F32) + l_main[1, :, sl].astype(F32)
        rows4 = jnp.concatenate(
            [jnp.where(jnp.logical_and(ln128 >= 32 * a, ln128 < 32 * a + 32), tot, zero) for a in range(4)], axis=0)
        res = dot(rows4.astype(BF16), f4t)
        for a in range(4):
            for k in range(2):
                hg[k, pl.ds(4 * g + a, SL, stride=I), :] = res[a * SL:(a + 1) * SL, k * 128:(k + 1) * 128]
    for t in range(2):
        hop_wait(rh.at[t], rhin.at[t], t, hop2_s, hop2_r.at[t])
    for m in range(4):
        dense = [jnp.concatenate([rhin[0, 3 * m + k], rhin[1, 3 * m + k]], axis=0).astype(F32) for k in range(3)]
        for k, both in enumerate(restore(*dense)):
            qp = 4 * m + k
            tq[pl.ds(2 * qp, SL, stride=Q), :] = both
            tq[pl.ds(2 * qp + 1, SL, stride=Q), :] = roll(both, 64)
    iden_i = eye(I, 128)
    lni = lanes((I, 128))

    def finish(b, _):
        rows = 4 * I
        at = pl.multiple_of(b * rows, rows)
        tj = dot_nt(iden_i, tq[pl.ds(pl.multiple_of(b * 128, 128), 128), :].astype(BF16))
        parts = [jnp.where(jnp.logical_and(lni >= 32 * a, lni < 32 * a + 32), tj, 0.0) for a in range(4)]
        right = dot(jnp.concatenate(parts, axis=0).astype(BF16), g4t)
        left = jnp.concatenate([hg[0, pl.ds(at, rows), :], hg[1, pl.ds(at, rows), :]], axis=1)
        grad = (left + right) * scale
        xn = xhat[pl.ds(at, rows), :]
        m1 = jnp.mean(grad, axis=-1, keepdims=True)
        m2 = jnp.mean(grad * xn, axis=-1, keepdims=True)
        res = (grad - m1 - xn * m2) * rstd[pl.ds(at, rows), :]
        slope_ref[pl.ds(b * 4, 4)] = res.astype(BF16).reshape(4, I, CH)
        return 0

    lax.fori_loop(0, SL // 4, finish, 0)

    def drain(t, _):
        a2a_copy(t).wait()
        return 0

    lax.fori_loop(0, COLS - 1, drain, 0)
    for ring in first + second[0] + second[1] + big[0] + big[1] + small + [l_ring, l_back, l_sibs, l_swap]:
        for copy in ring:
            copy.wait_send()
    own_copy().wait()
    for t in range(2):
        hop_sent(rhop.at[:, pl.ds(SK * t, SK), :], rin.at[half], t, hop_s, hop_r.at[half])
        hop_sent(rh.at[t], rhin.at[half], t, hop2_s, hop2_r.at[half])


def on_device(profile, pair, loss, former, latter, mixing, expand, shrink):
    vmem = pl.BlockSpec(memory_space=pltpu.VMEM)
    dma = pltpu.SemaphoreType.DMA
    return pl.pallas_call(
        kernel,
        out_shape=(
            jax.ShapeDtypeStruct((IB, J * COLS, C), BF16),
            jax.ShapeDtypeStruct((I, J, C), BF16),
            jax.ShapeDtypeStruct((SL, I, CH), BF16),
        ),
        in_specs=[vmem] * 8,
        out_specs=(pl.BlockSpec(memory_space=pl.ANY), vmem, vmem),
        scratch_shapes=[
            pltpu.VMEM((SL * I, CH), F32),
            pltpu.VMEM((SL * I, 1), F32),
            pltpu.VMEM((SL * I, 128), F32),
            pltpu.VMEM((SL * Q, 128), F32),
            pltpu.VMEM((S, I * Q), BF16),
            pltpu.VMEM((I * Q, S), BF16),
            pltpu.VMEM((12, SL, 128), BF16),
            pltpu.VMEM((2, 12, SK, 128), BF16),
            pltpu.VMEM((S, FULL), BF16),
            pltpu.VMEM((2, Q * Q, 8 * JP), BF16),
            pltpu.VMEM((I * Q, FULL), BF16),
            pltpu.VMEM((I, J, C), BF16),
            pltpu.VMEM((Q * Q, C), F32),
            pltpu.VMEM((Q * Q, C), BF16),
            pltpu.VMEM((C, Q * Q), BF16),
            pltpu.VMEM((H, C), BF16),
            pltpu.VMEM((C, H), BF16),
            pltpu.VMEM((S, I * Q), BF16),
            pltpu.VMEM((S, PK), BF16),
            pltpu.VMEM((2, 12, SK, 128), BF16),
            pltpu.VMEM((2, 12, SK, 128), BF16),
            pltpu.VMEM((2, SL * I, 128), F32),
            pltpu.VMEM((C, I * JP), BF16),
            pltpu.VMEM((C, I * JP), BF16),
            pltpu.VMEM((H, I * JP), BF16),
            pltpu.VMEM((2, 4, 2, SK, PK // 4), BF16),
            pltpu.VMEM((2, 4, 2, SK, PK // 2), BF16),
            pltpu.VMEM((2, 3, SK, PK // 2), BF16),
            pltpu.VMEM((2, SL, I * Q // 2), BF16),
            pltpu.VMEM((2, SL, I * Q), BF16),
            pltpu.VMEM((4, SL, I * Q), BF16),
            dma((2,)), dma((2,)),
            dma((11, 4)), dma((11, 4)),
            dma((8,)), dma((8,)),
            dma((COLS,)), dma((COLS,)),
            dma((11, 4)), dma((11, 4)),
            dma((2,)), dma((2,)),
        ],
        compiler_params=pltpu.CompilerParams(
            collective_id=0, has_side_effects=True, vmem_limit_bytes=60 * 1024 * 1024),
        cost_estimate=pl.CostEstimate(flops=16_000_000_000, bytes_accessed=8_000_000, transcendentals=3_000_000),
    )(profile, pair, loss, former.T, latter.T, mixing, expand, shrink)


def solution(mesh):
    return jax.shard_map(
        on_device,
        mesh=mesh,
        in_specs=(P("col", "row", None), P("row", "col", None), P("row", "col", None), P(), P(), P(), P(), P()),
        out_specs=(P(("row", "col"), None, None), P("row", "col", None), P("col", "row", None)),
        check_vma=False,
    )
```

```python
import functools

import jax
import jax.numpy as jnp
from jax import lax
from jax.experimental import pallas as pl
from jax.experimental.pallas import tpu as pltpu
from jax.sharding import PartitionSpec as P

MESH = pl.DeviceIdType.MESH
EPS = 1e-05
F32 = jnp.float32
BF16 = jnp.bfloat16

ROWS, COLS = 16, 8
S, SL = 256, 32
I, J, JP = 48, 96, 128
Q = 32
C, H, CH = 128, 512, 256
SK = S // ROWS
G8 = Q // 4
PK = 3 * G8 * 128
FULL = Q * JP
IB = I // COLS
HALF = FULL // 2
SLABS = sum(([4 * g + m for g in range(4 * k, 4 * k + 4) for m in range(3)]
             + [4 * g + 3 for g in range(4 * k, 4 * k + 4)] for k in range(2)), [])


def packed(g, m):
    at = (g // 4) * HALF + (3 * (g % 4) + m) * 128
    return slice(at, at + 128)


def fourth(g):
    at = (g // 4) * HALF + (12 + g % 4) * 128
    return slice(at, at + 128)


def dot(a, b):
    return jnp.dot(a, b, preferred_element_type=F32)


def dot_nt(a, b):
    return lax.dot_general(a, b, (((1,), (1,)), ((), ())), preferred_element_type=F32)


def eye(n, m=None):
    m = n if m is None else m
    i = lax.broadcasted_iota(jnp.int32, (n, m), 0)
    j = lax.broadcasted_iota(jnp.int32, (n, m), 1)
    return jnp.where(i == j, 1.0, 0.0).astype(BF16)


def lanes(shape):
    return lax.broadcasted_iota(jnp.int32, shape, 1)


def roll(x, shift):
    return pltpu.roll(x, shift, 1)


def pack4(q0, q1, q2, q3):
    ln = lanes(q0.shape)
    return (
        jnp.where(ln < 96, q0, roll(q3, 96)),
        jnp.where(ln < 96, q1, roll(q3, 64)),
        jnp.where(ln < 96, q2, roll(q3, 32)),
    )


def squeeze(t0, t1, t2, t3):
    inner = lax.rem(lanes(t0.shape), 64)
    return [jnp.where(inner < 48, t, roll(t3, 48 - 16 * k)) for k, t in enumerate((t0, t1, t2))]


def restore(t0, t1, t2):
    inner = lax.rem(lanes(t0.shape), 64)
    return [t0, t1, t2, jnp.where(inner < 16, roll(t0, 80), jnp.where(inner < 32, roll(t1, 96), roll(t2, 112)))]


def unpack_fourth(t0, t1, t2):
    ln = lanes(t0.shape)
    return jnp.where(ln < 32, roll(t0, 32), jnp.where(ln < 64, roll(t1, 64), roll(t2, 96)))


def kernel(
    x_ref, pair_ref, loss_ref, f_ref, g_ref, w_ref, e_ref, s_ref,
    out_ref, grad_ref, slope_ref,
    xhat, rstd, proj, tq, lall, lt, rhop, rin, rm, xs, acc, ogs, obuf,
    wf32, wf, wt, et, st, lgt, rgp, rh, rhin, hg, ct, lot, hgs, r_relay, r_main, r_small, l_relay, l_main, l_sib,
    hop_s, hop_r, ag_s, ag_r, sib_s, sib_r, a2a_s, a2a_r, rs_s, rs_r, hop2_s, hop2_r,
):
    r = lax.axis_index("row")
    c = lax.axis_index("col")
    half = lax.rem(r, 2)
    across = lax.div(r, 2)

    z, y = lax.div(r, 4), lax.rem(r, 4)
    x, core = lax.div(c, 2), lax.rem(c, 2)

    barrier = pltpu.get_barrier_semaphore()

    def at_row(z_, y_):
        return 4 * lax.rem(z_ + 4, 4) + lax.rem(y_ + 4, 4)

    def at_col(x_):
        return 2 * lax.rem(x_ + 4, 4) + core

    for row in (at_row(z - 1, y), at_row(z + 1, y), at_row(z + 2, y), at_row(z, y - 1), at_row(z, y + 1), at_row(z, y + 2)):
        pl.semaphore_signal(barrier, inc=1, device_id=(row, c), device_id_type=MESH)

    def greet_col(d, _):
        pl.semaphore_signal(barrier, inc=1, device_id=(r, lax.rem(c + d, COLS)), device_id_type=MESH)
        return 0

    lax.fori_loop(1, COLS, greet_col, 0)
    own = [jnp.logical_and(across == c, half == t) for t in range(2)]
    for t in range(2):
        @pl.when(jnp.logical_not(own[t]))
        def _():
            pl.semaphore_signal(barrier, inc=1, device_id=(2 * c + t, across), device_id_type=MESH)

    iden = eye(C)
    ln128 = lanes((SL, 128))
    tile4 = jnp.where(
        lax.rem(lax.broadcasted_iota(jnp.int32, (128, Q), 0), Q)
        == lax.broadcasted_iota(jnp.int32, (128, Q), 1), 1.0, 0.0).astype(BF16)
    f4t = dot(tile4, f_ref[...]).astype(BF16)
    g4t = dot(tile4, g_ref[...]).astype(BF16)
    tq[...] = jnp.zeros_like(tq)

    def project(b, _):
        rows = 4 * I
        at = pl.multiple_of(b * rows, rows)
        xr = x_ref[pl.ds(b * 4, 4)].reshape(rows, CH).astype(F32)
        center = xr - jnp.mean(xr, axis=-1, keepdims=True)
        inv = lax.rsqrt(jnp.mean(center * center, axis=-1, keepdims=True) + EPS)
        xn = center * inv
        xhat[pl.ds(at, rows), :] = xn
        rstd[pl.ds(at, rows), :] = inv
        xb = xn.astype(BF16)
        proj[pl.ds(at, rows), :] = dot_nt(xb, f4t)
        for k in range(4):
            to = pl.multiple_of((b * 4 + k) * Q, Q)
            tq[pl.ds(to, Q), 0:I] = dot_nt(g_ref[...], xb[k * I:(k + 1) * I])
        return 0

    lax.fori_loop(0, SL // 4, project, 0, unroll=4)

    mine = pl.ds(pl.multiple_of(c * SL, SL), SL)
    for m in range(4):
        pairs = []
        for qp in range(4 * m, 4 * m + 4):
            even = tq[pl.ds(2 * qp, SL, stride=Q), :]
            odd = tq[pl.ds(2 * qp + 1, SL, stride=Q), :]
            pairs.append(jnp.where(ln128 < 64, even, roll(odd, 64)))
        for k, tile in enumerate(squeeze(*pairs)):
            rhop[3 * m + k] = tile.astype(BF16)
    for g in range(I // 4):
        parts = [proj[pl.ds(4 * g + a, SL, stride=I), :] for a in range(4)]
        tile = jnp.where(ln128 < 32, parts[0], jnp.where(ln128 < 64, parts[1],
                         jnp.where(ln128 < 96, parts[2], parts[3])))
        lall[mine, g * 128:(g + 1) * 128] = tile.astype(BF16)

    pl.semaphore_wait(barrier, 6 + COLS - 1 + 2 - (across == c).astype(jnp.int32))

    def hop_remote(src, dst, t, ss, rs):
        return pltpu.make_async_remote_copy(
            src_ref=src, dst_ref=dst, send_sem=ss, recv_sem=rs,
            device_id=(2 * c + t, across), device_id_type=MESH)

    def hop_start(src, dst, t, ss, rs):
        @pl.when(own[t])
        def _():
            pltpu.make_async_copy(src, dst, rs).start()

        @pl.when(jnp.logical_not(own[t]))
        def _():
            hop_remote(src, dst, t, ss, rs).start()

    def hop_wait(src, dst, t, ss, rs):
        @pl.when(own[t])
        def _():
            pltpu.make_async_copy(src, dst, rs).wait()

        @pl.when(jnp.logical_not(own[t]))
        def _():
            hop_remote(src, dst, t, ss, rs).wait_recv()

    def hop_sent(src, dst, t, ss, rs):
        @pl.when(jnp.logical_not(own[t]))
        def _():
            hop_remote(src, dst, t, ss, rs).wait_send()

    def hop_out(k, t):
        return (rhop.at[pl.ds(6 * k, 6), pl.ds(SK * t, SK), :], rin.at[half, pl.ds(6 * k, 6)], t,
                hop_s.at[k, t], hop_r.at[k, half])

    def hop_in(k, t):
        return (rhop.at[pl.ds(6 * k, 6), pl.ds(SK * t, SK), :], rin.at[t, pl.ds(6 * k, 6)], t,
                hop_s.at[k, t], hop_r.at[k, t])

    def back_out(k, t):
        return (rh.at[t, pl.ds(6 * k, 6)], rhin.at[half, pl.ds(6 * k, 6)], t, hop2_s.at[k, t], hop2_r.at[k, half])

    def back_in(k, t):
        return (rh.at[t, pl.ds(6 * k, 6)], rhin.at[t, pl.ds(6 * k, 6)], t, hop2_s.at[k, t], hop2_r.at[k, t])

    for k in range(2):
        for t in range(2):
            hop_start(*hop_out(k, t))

    wf32[...] = w_ref[...].astype(F32)
    for k, q in enumerate(SLABS):
        wf[k * Q:(k + 1) * Q, :] = wf32[pl.ds(q, Q, stride=Q), :].astype(BF16)
    wt[...] = dot_nt(iden, wf[...]).astype(BF16)
    st[...] = dot_nt(iden, s_ref[...]).astype(BF16)
    et[...] = dot_nt(eye(H), e_ref[...]).astype(BF16)
    pad = jnp.zeros((JP - J, C), BF16)

    def ahead(k, _):
        to = pl.ds(pl.multiple_of(k * 256, 256), 256)
        pr = jnp.concatenate([pair_ref[2 * k], pad, pair_ref[2 * k + 1], pad], axis=0)
        lo = jnp.concatenate([loss_ref[2 * k], pad, loss_ref[2 * k + 1], pad], axis=0)
        ct[:, to] = pr.T
        lob = lo.T
        lot[:, to] = lob
        hgs[:, to] = dot(s_ref[...], lob).astype(BF16)
        return 0

    lax.fori_loop(0, 12, ahead, 0, unroll=6)

    ln16 = lanes((SK, 128))
    here = pl.ds(pl.multiple_of(r * SK, SK), SK)

    def assemble(k):
        loose = [sum((restore(*[rin[n, 3 * m + i].astype(F32) for i in range(3)]) for m in (2 * k, 2 * k + 1)), [])
                 for n in range(2)]
        for g in range(4):
            tiles = []
            for i in range(2):
                a, b = loose[0][2 * g + i], loose[1][2 * g + i]
                tiles.append(jnp.where(ln16 < 48, a, roll(b, 48)))
                tiles.append(jnp.where(ln16 < 48, roll(a, 64), roll(b, 112)))
            for m, tile in enumerate(pack4(*tiles)):
                rm[here, packed(4 * k + g, m)] = tile.astype(BF16)

    def send(src, dst, ss, rs, to):
        return pltpu.make_async_remote_copy(
            src_ref=src, dst_ref=dst, send_sem=ss, recv_sem=rs, device_id=to, device_id_type=MESH)

    def gather_ring(sl, to, g):
        return [
            send(sl(0, 0, 2), sl(0, 0, 2), ag_s.at[g, 0], ag_r.at[g, 0], to(1)),
            send(sl(0, 0, 2), sl(0, 0, 2), ag_s.at[g, 1], ag_r.at[g, 1], to(-1)),
            send(sl(-1, 0, 1), sl(-1, 0, 1), ag_s.at[g, 2], ag_r.at[g, 2], to(1)),
            send(sl(1, 1, 1), sl(1, 1, 1), ag_s.at[g, 3], ag_r.at[g, 3], to(-1)),
        ]

    def gather_direct(sl, to, g):
        return [send(sl(0, 0, 2), sl(0, 0, 2), ag_s.at[g, k], ag_r.at[g, k], to(d)) for k, d in enumerate((1, -1, 2))]

    def scatter_direct(sl, into, to, g):
        return [send(sl(d, 0, 2), into.at[k], rs_s.at[g, k], rs_r.at[g, k], to(d)) for k, d in enumerate((1, -1, 2))]

    def scatter_ring(sl, relay, main, to, g):
        return [
            send(sl(2, 0, 1), relay.at[0], rs_s.at[g, 0], rs_r.at[g, 0], to(1)),
            send(sl(2, 1, 1), relay.at[1], rs_s.at[g, 1], rs_r.at[g, 1], to(-1)),
            send(sl(1, 0, 2), main.at[0], rs_s.at[g, 2], rs_r.at[g, 2], to(1)),
            send(sl(-1, 0, 2), main.at[1], rs_s.at[g, 3], rs_r.at[g, 3], to(-1)),
        ]

    def chunk(ref, side, along_z, w):
        def sl(off, first, count):
            row = at_row(z + off, y + w) if along_z else at_row(z + w, y + off)
            return ref.at[pl.ds(pl.multiple_of(row * SK, SK), SK),
                          pl.ds(side * (HALF if ref is rm else PK // 2) + first * (PK // 4), count * (PK // 4))]
        return sl

    def along(along_z):
        return lambda d: (at_row(z + d, y), c) if along_z else (at_row(z, y + d), c)

    def l_chunk(ref):
        def sl(off, first, count):
            return ref.at[pl.ds(pl.multiple_of(at_col(x + off) * SL, SL), SL), pl.ds(first * (I * Q // 2), count * (I * Q // 2))]
        return sl

    def to_x(d):
        return (r, at_col(x + d))

    sibling = (r, c + 1 - 2 * core)
    STEPS = (0, -1, 1, 2)
    first = [gather_direct(chunk(rm, k, k == 1, 0), along(k == 1), 5 * k) for k in range(2)]
    second = [[gather_ring(chunk(rm, k, k == 0, w), along(k == 0), 5 * k + 1 + n)
               for n, w in enumerate(STEPS)] for k in range(2)]
    l_ring = gather_ring(l_chunk(lall), to_x, 10)
    l_sibs = [send(l_chunk(lall)(w, 0, 2), l_chunk(lall)(w, 0, 2), sib_s.at[n], sib_r.at[n], sibling)
              for n, w in enumerate(STEPS)]
    for k in range(2):
        for t in range(2):
            hop_wait(*hop_in(k, t))
        assemble(k)
        for copy in first[k] + second[k][0][:2]:
            copy.start()
    l_ring[0].start()
    l_ring[1].start()
    l_sibs[0].start()
    lax.fori_loop(12, 15, ahead, 0, unroll=3)
    for k in range(2):
        for m in range(3):
            first[k][m].wait_recv()
            second[k][1 + m][0].start()
            second[k][1 + m][1].start()
    lax.fori_loop(15, 18, ahead, 0, unroll=3)
    for m in range(2):
        l_ring[m].wait_recv()
        l_ring[2 + m].start()
        l_sibs[1 + m].start()
    for k in range(2):
        for n in range(4):
            for m in range(2):
                second[k][n][m].wait_recv()
                second[k][n][2 + m].start()
        lax.fori_loop(18 + 3 * k, 21 + 3 * k, ahead, 0, unroll=3)
    l_ring[2].wait_recv()
    l_ring[3].wait_recv()
    l_sibs[3].start()
    for n in range(4):
        l_sibs[n].wait_recv()
    for k in range(I * Q // S):
        lt[k * S:(k + 1) * S, :] = lall[:, k * S:(k + 1) * S].T
    scale = 1.0 / S

    def mix(side, b):
        for k in range(2):
            at = pl.multiple_of((2 * b + k) * 256, 256)
            ltb = lt[pl.ds(at, 256), :]
            for ch in range(4):
                d = dot(ltb, rm[:, side * HALF + ch * 512:side * HALF + (ch + 1) * 512]).astype(BF16)
                for m in range(4):
                    slab = ch * 4 + m
                    for i in range(8):
                        xs[k, slab * Q:(slab + 1) * Q, i * JP:(i + 1) * JP] = d[i * Q:(i + 1) * Q, m * 128:(m + 1) * 128]
        for k in range(2):
            to = pl.ds(pl.multiple_of((2 * b + k) * 1024, 1024), 1024)
            part = dot(wt[:, side * 512:(side + 1) * 512], xs[k])
            if side == 0:
                acc[:, to] = part
            else:
                ct[:, to] = (ct[:, to].astype(F32) + (acc[:, to] + part) * scale).astype(BF16)
        return 0

    for k in range(2):
        for n in range(4):
            second[k][n][2].wait_recv()
            second[k][n][3].wait_recv()
        for g in range(4 * k, 4 * k + 4):
            rm[:, fourth(g)] = unpack_fourth(*[rm[:, packed(g, m)].astype(F32) for m in range(3)]).astype(BF16)
        lax.fori_loop(0, I // 16, lambda b, _: mix(k, b), 0)

    def a2a_copy(t):
        to = lax.rem(c + 1 + t, COLS)
        return pltpu.make_async_remote_copy(
            src_ref=obuf.at[pl.ds(to * IB, IB)], dst_ref=out_ref.at[:, pl.ds(pl.multiple_of(c * J, J), J), :],
            send_sem=a2a_s.at[t], recv_sem=a2a_r.at[t], device_id=(r, to), device_id_type=MESH)

    def own_copy():
        return pltpu.make_async_copy(
            obuf.at[pl.ds(c * IB, IB)], out_ref.at[:, pl.ds(pl.multiple_of(c * J, J), J), :],
            a2a_s.at[COLS - 1])

    def block(t, _):
        ib = lax.rem(c + 1 + t, COLS)
        for half_block in range(IB // 2):
            i0 = ib * IB + 2 * half_block
            here_l = pl.ds(pl.multiple_of(i0 * JP, 2 * JP), 2 * JP)
            mid = ct[:, here_l].astype(F32)
            center = mid - jnp.mean(mid, axis=0, keepdims=True)
            inv = lax.rsqrt(jnp.mean(center * center, axis=0, keepdims=True) + EPS)
            xn = center * inv
            pre = dot(et[...], xn.astype(BF16))
            hgr = hgs[:, here_l].astype(F32)
            sg = 0.5 * jnp.tanh(0.5 * pre) + 0.5
            hid = pre * sg
            pgr = (hgr * (sg + hid * (1.0 - sg))).astype(BF16)
            outb = (mid + dot(st[...], hid.astype(BF16))).astype(BF16)
            hatg = dot(e_ref[...], pgr)
            m1 = jnp.mean(hatg, axis=0, keepdims=True)
            m2 = jnp.mean(hatg * xn, axis=0, keepdims=True)
            gb = (lot[:, here_l].astype(F32) + (hatg - m1 - xn * m2) * inv).astype(BF16)
            for i in range(2):
                sl = slice(i * JP, (i + 1) * JP)
                obuf[i0 + i] = outb[:, sl].T[0:J]
                grad_ref[i0 + i] = gb[:, sl].T[0:J]
            og = dot(wf[...], gb).astype(BF16)
            for i in range(2):
                to = pl.ds(pl.multiple_of((i0 + i) * Q, Q), Q)
                for k in range(Q):
                    ogs[to, k * 128:(k + 1) * 128] = og[k * Q:(k + 1) * Q, i * JP:(i + 1) * JP]

        @pl.when(t < COLS - 1)
        def _():
            a2a_copy(t).start()

        @pl.when(t == COLS - 1)
        def _():
            own_copy().start()

        return 0

    lax.fori_loop(0, COLS, block, 0, unroll=2)

    big = [[scatter_ring(chunk(rgp, k, k == 0, w), r_relay.at[k, n], r_main.at[k, n], along(k == 0), 5 * k + n)
            for n, w in enumerate(STEPS)] for k in range(2)]
    small = [scatter_direct(chunk(rgp, k, k == 1, 0), r_small.at[k], along(k == 1), 5 * k + 4)
             for k in range(2)]
    for g in range(0, G8, 2):
        a = dot(lall[...], ogs[:, packed(g, 0).start:packed(g + 1, 2).stop])
        b = dot(lall[...], ogs[:, fourth(g).start:fourth(g + 1).stop])
        for k in range(2):
            tiles = pack4(*[a[:, (3 * k + m) * 128:(3 * k + m + 1) * 128] for m in range(3)],
                          b[:, k * 128:(k + 1) * 128])
            for m in range(3):
                at = (3 * (g + k) + m) * 128
                rgp[:, at:at + 128] = tiles[m].astype(BF16)
        if g % 4 == 2:
            for n in range(4):
                big[g // 4][n][0].start()
                big[g // 4][n][1].start()

    def add(dst, *srcs):
        tot = dst[...].astype(F32)
        for src in srcs:
            tot = tot + src[...].astype(F32)
        dst[...] = tot.astype(BF16)

    def left_grad(k):
        lgt[:, k * S:(k + 1) * S] = dot_nt(rm[...], ogs[k * S:(k + 1) * S, :]).astype(BF16)

    def relayed(ring, sl, relay):
        ring[0].wait_recv()
        add(sl(1, 0, 1), relay.at[0])
        ring[2].start()
        ring[1].wait_recv()
        add(sl(-1, 1, 1), relay.at[1])
        ring[3].start()

    left_grad(0)
    for n, w in enumerate(STEPS):
        for k in range(2):
            relayed(big[k][n], chunk(rgp, k, k == 0, w), r_relay.at[k, n])
    for k in range(1, I * Q // S):
        left_grad(k)
    l_swap = [send(lgt.at[pl.ds(pl.multiple_of((2 * n + 1 - core) * SL, SL), SL)], l_sib.at[n],
                   sib_s.at[4 + n], sib_r.at[4 + n], sibling) for n in range(4)]
    for n in range(4):
        l_swap[n].start()
    for k in range(2):
        for n, w in enumerate(STEPS):
            big[k][n][2].wait_recv()
            big[k][n][3].wait_recv()
            add(chunk(rgp, k, k == 0, w)(0, 0, 2), r_main.at[k, n, 0], r_main.at[k, n, 1])
        for copy in small[k]:
            copy.start()
    for n in range(4):
        l_swap[n].wait_recv()
        add(lgt.at[pl.ds(pl.multiple_of((2 * n + core) * SL, SL), SL)], l_sib.at[n])
    l_back = scatter_ring(l_chunk(lgt), l_relay, l_main, to_x, 10)
    l_back[0].start()
    l_back[1].start()

    def hand_back(k):
        for copy in small[k]:
            copy.wait_recv()
        loose = [[], []]
        for g in range(4 * k, 4 * k + 4):
            tiles = []
            for m in range(3):
                at = (3 * g + m) * 128
                sl = slice(at - k * (PK // 2), at - k * (PK // 2) + 128)
                tot = rgp[here, at:at + 128].astype(F32)
                for n in range(3):
                    tot = tot + r_small[k, n, :, sl].astype(F32)
                tiles.append(tot)
            tiles.append(unpack_fourth(*tiles))
            for i in range(2):
                even, odd = tiles[2 * i], tiles[2 * i + 1]
                loose[0].append(jnp.where(ln16 < 64, even, roll(odd, 64)))
                loose[1].append(jnp.where(ln16 < 64, roll(even, 80), roll(odd, 16)))
        for n in range(2):
            for m in range(2):
                for i, tile in enumerate(squeeze(*loose[n][4 * m:4 * m + 4])):
                    rh[n, 6 * k + 3 * m + i] = tile.astype(BF16)
        for t in range(2):
            hop_start(*back_out(k, t))

    hand_back(0)
    relayed(l_back, l_chunk(lgt), l_relay)
    hand_back(1)
    l_back[2].wait_recv()
    l_back[3].wait_recv()
    zero = jnp.zeros((SL, 128), F32)
    for g in range(I // 4):
        sl = slice(g * 128, (g + 1) * 128)
        tot = lgt[mine, sl].astype(F32) + l_main[0, :, sl].astype(F32) + l_main[1, :, sl].astype(F32)
        rows4 = jnp.concatenate(
            [jnp.where(jnp.logical_and(ln128 >= 32 * a, ln128 < 32 * a + 32), tot, zero) for a in range(4)], axis=0)
        res = dot(rows4.astype(BF16), f4t)
        for a in range(4):
            for k in range(2):
                hg[k, pl.ds(4 * g + a, SL, stride=I), :] = res[a * SL:(a + 1) * SL, k * 128:(k + 1) * 128]
    for k in range(2):
        for t in range(2):
            hop_wait(*back_in(k, t))
    for m in range(4):
        dense = [jnp.concatenate([rhin[0, 3 * m + k], rhin[1, 3 * m + k]], axis=0).astype(F32) for k in range(3)]
        for k, both in enumerate(restore(*dense)):
            qp = 4 * m + k
            tq[pl.ds(2 * qp, SL, stride=Q), :] = both
            tq[pl.ds(2 * qp + 1, SL, stride=Q), :] = roll(both, 64)
    iden_i = eye(I, 128)
    lni = lanes((I, 128))

    def finish(b, _):
        rows = 4 * I
        at = pl.multiple_of(b * rows, rows)
        tj = dot_nt(iden_i, tq[pl.ds(pl.multiple_of(b * 128, 128), 128), :].astype(BF16))
        parts = [jnp.where(jnp.logical_and(lni >= 32 * a, lni < 32 * a + 32), tj, 0.0) for a in range(4)]
        right = dot(jnp.concatenate(parts, axis=0).astype(BF16), g4t)
        left = jnp.concatenate([hg[0, pl.ds(at, rows), :], hg[1, pl.ds(at, rows), :]], axis=1)
        grad = (left + right) * scale
        xn = xhat[pl.ds(at, rows), :]
        m1 = jnp.mean(grad, axis=-1, keepdims=True)
        m2 = jnp.mean(grad * xn, axis=-1, keepdims=True)
        res = (grad - m1 - xn * m2) * rstd[pl.ds(at, rows), :]
        slope_ref[pl.ds(b * 4, 4)] = res.astype(BF16).reshape(4, I, CH)
        return 0

    lax.fori_loop(0, SL // 4, finish, 0, unroll=4)

    def drain(t, _):
        a2a_copy(t).wait()
        return 0

    lax.fori_loop(0, COLS - 1, drain, 0)
    for ring in first + second[0] + second[1] + big[0] + big[1] + small + [l_ring, l_back, l_sibs, l_swap]:
        for copy in ring:
            copy.wait_send()
    own_copy().wait()
    for k in range(2):
        for t in range(2):
            hop_sent(*hop_out(k, t))
            hop_sent(*back_out(k, t))


def on_device(profile, pair, loss, former, latter, mixing, expand, shrink):
    vmem = pl.BlockSpec(memory_space=pltpu.VMEM)
    dma = pltpu.SemaphoreType.DMA
    return pl.pallas_call(
        kernel,
        out_shape=(
            jax.ShapeDtypeStruct((IB, J * COLS, C), BF16),
            jax.ShapeDtypeStruct((I, J, C), BF16),
            jax.ShapeDtypeStruct((SL, I, CH), BF16),
        ),
        in_specs=[vmem] * 8,
        out_specs=(pl.BlockSpec(memory_space=pl.ANY), vmem, vmem),
        scratch_shapes=[
            pltpu.VMEM((SL * I, CH), F32),
            pltpu.VMEM((SL * I, 1), F32),
            pltpu.VMEM((SL * I, 128), F32),
            pltpu.VMEM((SL * Q, 128), F32),
            pltpu.VMEM((S, I * Q), BF16),
            pltpu.VMEM((I * Q, S), BF16),
            pltpu.VMEM((12, SL, 128), BF16),
            pltpu.VMEM((2, 12, SK, 128), BF16),
            pltpu.VMEM((S, FULL), BF16),
            pltpu.VMEM((2, Q * Q // 2, 8 * JP), BF16),
            pltpu.VMEM((C, I * JP), F32),
            pltpu.VMEM((I * Q, FULL), BF16),
            pltpu.VMEM((I, J, C), BF16),
            pltpu.VMEM((Q * Q, C), F32),
            pltpu.VMEM((Q * Q, C), BF16),
            pltpu.VMEM((C, Q * Q), BF16),
            pltpu.VMEM((H, C), BF16),
            pltpu.VMEM((C, H), BF16),
            pltpu.VMEM((S, I * Q), BF16),
            pltpu.VMEM((S, PK), BF16),
            pltpu.VMEM((2, 12, SK, 128), BF16),
            pltpu.VMEM((2, 12, SK, 128), BF16),
            pltpu.VMEM((2, SL * I, 128), F32),
            pltpu.VMEM((C, I * JP), BF16),
            pltpu.VMEM((C, I * JP), BF16),
            pltpu.VMEM((H, I * JP), BF16),
            pltpu.VMEM((2, 4, 2, SK, PK // 4), BF16),
            pltpu.VMEM((2, 4, 2, SK, PK // 2), BF16),
            pltpu.VMEM((2, 3, SK, PK // 2), BF16),
            pltpu.VMEM((2, SL, I * Q // 2), BF16),
            pltpu.VMEM((2, SL, I * Q), BF16),
            pltpu.VMEM((4, SL, I * Q), BF16),
            dma((2, 2)), dma((2, 2)),
            dma((11, 4)), dma((11, 4)),
            dma((8,)), dma((8,)),
            dma((COLS,)), dma((COLS,)),
            dma((11, 4)), dma((11, 4)),
            dma((2, 2)), dma((2, 2)),
        ],
        compiler_params=pltpu.CompilerParams(
            collective_id=0, has_side_effects=True, vmem_limit_bytes=60 * 1024 * 1024),
        cost_estimate=pl.CostEstimate(flops=16_000_000_000, bytes_accessed=8_000_000, transcendentals=3_000_000),
    )(profile, pair, loss, former.T, latter.T, mixing, expand, shrink)


def solution(mesh):
    return jax.shard_map(
        on_device,
        mesh=mesh,
        in_specs=(P("col", "row", None), P("row", "col", None), P("row", "col", None), P(), P(), P(), P(), P()),
        out_specs=(P(("row", "col"), None, None), P("row", "col", None), P("col", "row", None)),
        check_vma=False,
    )
```

```python
import functools

import jax
import jax.numpy as jnp
from jax import lax
from jax.experimental import pallas as pl
from jax.experimental.pallas import tpu as pltpu
from jax.sharding import PartitionSpec as P

MESH = pl.DeviceIdType.MESH
EPS = 1e-05
F32 = jnp.float32
BF16 = jnp.bfloat16

ROWS, COLS = 16, 8
S, SL = 256, 32
I, J, JP = 48, 96, 128
Q = 32
C, H, CH = 128, 512, 256
SK = S // ROWS
G8 = Q // 4
PK = 3 * G8 * 128
FULL = Q * JP
IB = I // COLS
HALF = FULL // 2
SLABS = sum(([4 * g + m for g in range(4 * k, 4 * k + 4) for m in range(3)]
             + [4 * g + 3 for g in range(4 * k, 4 * k + 4)] for k in range(2)), [])


def packed(g, m):
    at = (g // 4) * HALF + (3 * (g % 4) + m) * 128
    return slice(at, at + 128)


def fourth(g):
    at = (g // 4) * HALF + (12 + g % 4) * 128
    return slice(at, at + 128)


def dot(a, b):
    return jnp.dot(a, b, preferred_element_type=F32)


def dot_nt(a, b):
    return lax.dot_general(a, b, (((1,), (1,)), ((), ())), preferred_element_type=F32)


def eye(n, m=None):
    m = n if m is None else m
    i = lax.broadcasted_iota(jnp.int32, (n, m), 0)
    j = lax.broadcasted_iota(jnp.int32, (n, m), 1)
    return jnp.where(i == j, 1.0, 0.0).astype(BF16)


def lanes(shape):
    return lax.broadcasted_iota(jnp.int32, shape, 1)


def roll(x, shift):
    return pltpu.roll(x, shift, 1)


def pack4(q0, q1, q2, q3):
    ln = lanes(q0.shape)
    return (
        jnp.where(ln < 96, q0, roll(q3, 96)),
        jnp.where(ln < 96, q1, roll(q3, 64)),
        jnp.where(ln < 96, q2, roll(q3, 32)),
    )


def squeeze(t0, t1, t2, t3):
    inner = lax.rem(lanes(t0.shape), 64)
    return [jnp.where(inner < 48, t, roll(t3, 48 - 16 * k)) for k, t in enumerate((t0, t1, t2))]


def restore(t0, t1, t2):
    inner = lax.rem(lanes(t0.shape), 64)
    return [t0, t1, t2, jnp.where(inner < 16, roll(t0, 80), jnp.where(inner < 32, roll(t1, 96), roll(t2, 112)))]


def unpack_fourth(t0, t1, t2):
    ln = lanes(t0.shape)
    return jnp.where(ln < 32, roll(t0, 32), jnp.where(ln < 64, roll(t1, 64), roll(t2, 96)))


def tile_rows():
    return jnp.where(
        lax.rem(lax.broadcasted_iota(jnp.int32, (128, Q), 0), Q)
        == lax.broadcasted_iota(jnp.int32, (128, Q), 1), 1.0, 0.0).astype(BF16)


def normalise(x_ref, b):
    xr = x_ref[pl.ds(b * 4, 4)].reshape(4 * I, CH).astype(F32)
    center = xr - jnp.mean(xr, axis=-1, keepdims=True)
    inv = lax.rsqrt(jnp.mean(center * center, axis=-1, keepdims=True) + EPS)
    return center * inv, inv


def kernel(
    x_ref, pair_hbm, loss_hbm, f_ref, g_ref, w_ref, e_ref, s_ref,
    out_ref, grad_hbm, ltot_ref, tq_ref,
    pair_ref, loss_ref, gbuf, proj, tq, lall, lt, rhop, rin, rm, xs, acc, ogs, obuf,
    wf32, wf, wt, et, st, lgt, rgp, rh, rhin, ct, lot, hgs, r_relay, r_main, r_small, l_relay, l_main, l_sib,
    io_s, hop_s, hop_r, ag_s, ag_r, sib_s, sib_r, a2a_s, a2a_r, rs_s, rs_r, hop2_s, hop2_r,
):
    r = lax.axis_index("row")
    c = lax.axis_index("col")
    half = lax.rem(r, 2)
    across = lax.div(r, 2)

    z, y = lax.div(r, 4), lax.rem(r, 4)
    fetch = [pltpu.make_async_copy(pair_hbm, pair_ref, io_s.at[0]), pltpu.make_async_copy(loss_hbm, loss_ref, io_s.at[1])]
    for copy in fetch:
        copy.start()
    x, core = lax.div(c, 2), lax.rem(c, 2)

    barrier = pltpu.get_barrier_semaphore()

    def at_row(z_, y_):
        return 4 * lax.rem(z_ + 4, 4) + lax.rem(y_ + 4, 4)

    def at_col(x_):
        return 2 * lax.rem(x_ + 4, 4) + core

    for row in (at_row(z - 1, y), at_row(z + 1, y), at_row(z + 2, y), at_row(z, y - 1), at_row(z, y + 1), at_row(z, y + 2)):
        pl.semaphore_signal(barrier, inc=1, device_id=(row, c), device_id_type=MESH)

    def greet_col(d, _):
        pl.semaphore_signal(barrier, inc=1, device_id=(r, lax.rem(c + d, COLS)), device_id_type=MESH)
        return 0

    lax.fori_loop(1, COLS, greet_col, 0)
    own = [jnp.logical_and(across == c, half == t) for t in range(2)]
    for t in range(2):
        @pl.when(jnp.logical_not(own[t]))
        def _():
            pl.semaphore_signal(barrier, inc=1, device_id=(2 * c + t, across), device_id_type=MESH)

    iden = eye(C)
    ln128 = lanes((SL, 128))
    f4t = dot(tile_rows(), f_ref[...]).astype(BF16)
    tq[...] = jnp.zeros_like(tq)

    def project(b, _):
        rows = 4 * I
        at = pl.multiple_of(b * rows, rows)
        xn = normalise(x_ref, b)[0]
        xb = xn.astype(BF16)
        proj[pl.ds(at, rows), :] = dot_nt(xb, f4t)
        for k in range(4):
            to = pl.multiple_of((b * 4 + k) * Q, Q)
            tq[pl.ds(to, Q), 0:I] = dot_nt(g_ref[...], xb[k * I:(k + 1) * I])
        return 0

    lax.fori_loop(0, SL // 4, project, 0, unroll=4)

    mine = pl.ds(pl.multiple_of(c * SL, SL), SL)
    for m in range(4):
        pairs = []
        for qp in range(4 * m, 4 * m + 4):
            even = tq[pl.ds(2 * qp, SL, stride=Q), :]
            odd = tq[pl.ds(2 * qp + 1, SL, stride=Q), :]
            pairs.append(jnp.where(ln128 < 64, even, roll(odd, 64)))
        for k, tile in enumerate(squeeze(*pairs)):
            rhop[3 * m + k] = tile.astype(BF16)
    for g in range(I // 4):
        parts = [proj[pl.ds(4 * g + a, SL, stride=I), :] for a in range(4)]
        tile = jnp.where(ln128 < 32, parts[0], jnp.where(ln128 < 64, parts[1],
                         jnp.where(ln128 < 96, parts[2], parts[3])))
        lall[mine, g * 128:(g + 1) * 128] = tile.astype(BF16)

    pl.semaphore_wait(barrier, 6 + COLS - 1 + 2 - (across == c).astype(jnp.int32))

    def hop_remote(src, dst, t, ss, rs):
        return pltpu.make_async_remote_copy(
            src_ref=src, dst_ref=dst, send_sem=ss, recv_sem=rs,
            device_id=(2 * c + t, across), device_id_type=MESH)

    def hop_start(src, dst, t, ss, rs):
        @pl.when(own[t])
        def _():
            pltpu.make_async_copy(src, dst, rs).start()

        @pl.when(jnp.logical_not(own[t]))
        def _():
            hop_remote(src, dst, t, ss, rs).start()

    def hop_wait(src, dst, t, ss, rs):
        @pl.when(own[t])
        def _():
            pltpu.make_async_copy(src, dst, rs).wait()

        @pl.when(jnp.logical_not(own[t]))
        def _():
            hop_remote(src, dst, t, ss, rs).wait_recv()

    def hop_sent(src, dst, t, ss, rs):
        @pl.when(jnp.logical_not(own[t]))
        def _():
            hop_remote(src, dst, t, ss, rs).wait_send()

    def hop_out(k, t):
        return (rhop.at[pl.ds(6 * k, 6), pl.ds(SK * t, SK), :], rin.at[half, pl.ds(6 * k, 6)], t,
                hop_s.at[k, t], hop_r.at[k, half])

    def hop_in(k, t):
        return (rhop.at[pl.ds(6 * k, 6), pl.ds(SK * t, SK), :], rin.at[t, pl.ds(6 * k, 6)], t,
                hop_s.at[k, t], hop_r.at[k, t])

    def back_out(k, t):
        return (rh.at[t, pl.ds(6 * k, 6)], rhin.at[half, pl.ds(6 * k, 6)], t, hop2_s.at[k, t], hop2_r.at[k, half])

    def back_in(k, t):
        return (rh.at[t, pl.ds(6 * k, 6)], rhin.at[t, pl.ds(6 * k, 6)], t, hop2_s.at[k, t], hop2_r.at[k, t])

    for k in range(2):
        for t in range(2):
            hop_start(*hop_out(k, t))

    wf32[...] = w_ref[...].astype(F32)
    for k, q in enumerate(SLABS):
        wf[k * Q:(k + 1) * Q, :] = wf32[pl.ds(q, Q, stride=Q), :].astype(BF16)
    wt[...] = dot_nt(iden, wf[...]).astype(BF16)
    st[...] = dot_nt(iden, s_ref[...]).astype(BF16)
    et[...] = dot_nt(eye(H), e_ref[...]).astype(BF16)
    pad = jnp.zeros((JP - J, C), BF16)
    for copy in fetch:
        copy.wait()

    def ahead(k, _):
        to = pl.ds(pl.multiple_of(k * 256, 256), 256)
        pr = jnp.concatenate([pair_ref[2 * k], pad, pair_ref[2 * k + 1], pad], axis=0)
        lo = jnp.concatenate([loss_ref[2 * k], pad, loss_ref[2 * k + 1], pad], axis=0)
        ct[:, to] = pr.T
        lob = lo.T
        lot[:, to] = lob
        hgs[:, to] = dot(s_ref[...], lob).astype(BF16)
        return 0

    lax.fori_loop(0, 12, ahead, 0, unroll=6)

    ln16 = lanes((SK, 128))
    here = pl.ds(pl.multiple_of(r * SK, SK), SK)

    def assemble(k):
        loose = [sum((restore(*[rin[n, 3 * m + i].astype(F32) for i in range(3)]) for m in (2 * k, 2 * k + 1)), [])
                 for n in range(2)]
        for g in range(4):
            tiles = []
            for i in range(2):
                a, b = loose[0][2 * g + i], loose[1][2 * g + i]
                tiles.append(jnp.where(ln16 < 48, a, roll(b, 48)))
                tiles.append(jnp.where(ln16 < 48, roll(a, 64), roll(b, 112)))
            for m, tile in enumerate(pack4(*tiles)):
                rm[here, packed(4 * k + g, m)] = tile.astype(BF16)

    def send(src, dst, ss, rs, to):
        return pltpu.make_async_remote_copy(
            src_ref=src, dst_ref=dst, send_sem=ss, recv_sem=rs, device_id=to, device_id_type=MESH)

    def gather_ring(sl, to, g):
        return [
            send(sl(0, 0, 2), sl(0, 0, 2), ag_s.at[g, 0], ag_r.at[g, 0], to(1)),
            send(sl(0, 0, 2), sl(0, 0, 2), ag_s.at[g, 1], ag_r.at[g, 1], to(-1)),
            send(sl(-1, 0, 1), sl(-1, 0, 1), ag_s.at[g, 2], ag_r.at[g, 2], to(1)),
            send(sl(1, 1, 1), sl(1, 1, 1), ag_s.at[g, 3], ag_r.at[g, 3], to(-1)),
        ]

    def gather_direct(sl, to, g):
        return [send(sl(0, 0, 2), sl(0, 0, 2), ag_s.at[g, k], ag_r.at[g, k], to(d)) for k, d in enumerate((1, -1, 2))]

    def scatter_direct(sl, into, to, g):
        return [send(sl(d, 0, 2), into.at[k], rs_s.at[g, k], rs_r.at[g, k], to(d)) for k, d in enumerate((1, -1, 2))]

    def scatter_ring(sl, relay, main, to, g):
        return [
            send(sl(2, 0, 1), relay.at[0], rs_s.at[g, 0], rs_r.at[g, 0], to(1)),
            send(sl(2, 1, 1), relay.at[1], rs_s.at[g, 1], rs_r.at[g, 1], to(-1)),
            send(sl(1, 0, 2), main.at[0], rs_s.at[g, 2], rs_r.at[g, 2], to(1)),
            send(sl(-1, 0, 2), main.at[1], rs_s.at[g, 3], rs_r.at[g, 3], to(-1)),
        ]

    def chunk(ref, side, along_z, w):
        def sl(off, first, count):
            row = at_row(z + off, y + w) if along_z else at_row(z + w, y + off)
            return ref.at[pl.ds(pl.multiple_of(row * SK, SK), SK),
                          pl.ds(side * (HALF if ref is rm else PK // 2) + first * (PK // 4), count * (PK // 4))]
        return sl

    def along(along_z):
        return lambda d: (at_row(z + d, y), c) if along_z else (at_row(z, y + d), c)

    def l_chunk(ref):
        def sl(off, first, count):
            return ref.at[pl.ds(pl.multiple_of(at_col(x + off) * SL, SL), SL), pl.ds(first * (I * Q // 2), count * (I * Q // 2))]
        return sl

    def to_x(d):
        return (r, at_col(x + d))

    sibling = (r, c + 1 - 2 * core)
    STEPS = (0, -1, 1, 2)
    first = [gather_direct(chunk(rm, k, k == 1, 0), along(k == 1), 5 * k) for k in range(2)]
    second = [[gather_ring(chunk(rm, k, k == 0, w), along(k == 0), 5 * k + 1 + n)
               for n, w in enumerate(STEPS)] for k in range(2)]
    l_ring = gather_ring(l_chunk(lall), to_x, 10)
    l_sibs = [send(l_chunk(lall)(w, 0, 2), l_chunk(lall)(w, 0, 2), sib_s.at[n], sib_r.at[n], sibling)
              for n, w in enumerate(STEPS)]
    for k in range(2):
        for t in range(2):
            hop_wait(*hop_in(k, t))
        assemble(k)
        for copy in first[k] + second[k][0][:2]:
            copy.start()
    l_ring[0].start()
    l_ring[1].start()
    l_sibs[0].start()
    lax.fori_loop(12, 15, ahead, 0, unroll=3)
    for k in range(2):
        for m in range(3):
            first[k][m].wait_recv()
            second[k][1 + m][0].start()
            second[k][1 + m][1].start()
    lax.fori_loop(15, 18, ahead, 0, unroll=3)
    for m in range(2):
        l_ring[m].wait_recv()
        l_ring[2 + m].start()
        l_sibs[1 + m].start()
    for k in range(2):
        for n in range(4):
            for m in range(2):
                second[k][n][m].wait_recv()
                second[k][n][2 + m].start()
        lax.fori_loop(18 + 3 * k, 21 + 3 * k, ahead, 0, unroll=3)
    l_ring[2].wait_recv()
    l_ring[3].wait_recv()
    l_sibs[3].start()
    for n in range(4):
        l_sibs[n].wait_recv()
    for k in range(I * Q // S):
        lt[k * S:(k + 1) * S, :] = lall[:, k * S:(k + 1) * S].T
    scale = 1.0 / S

    def mix(side, b):
        for k in range(2):
            at = pl.multiple_of((2 * b + k) * 256, 256)
            ltb = lt[pl.ds(at, 256), :]
            for ch in range(4):
                d = dot(ltb, rm[:, side * HALF + ch * 512:side * HALF + (ch + 1) * 512]).astype(BF16)
                for m in range(4):
                    slab = ch * 4 + m
                    for i in range(8):
                        xs[k, slab * Q:(slab + 1) * Q, i * JP:(i + 1) * JP] = d[i * Q:(i + 1) * Q, m * 128:(m + 1) * 128]
        for k in range(2):
            to = pl.ds(pl.multiple_of((2 * b + k) * 1024, 1024), 1024)
            part = dot(wt[:, side * 512:(side + 1) * 512], xs[k])
            if side == 0:
                acc[:, to] = part
            else:
                ct[:, to] = (ct[:, to].astype(F32) + (acc[:, to] + part) * scale).astype(BF16)
        return 0

    for k in range(2):
        for n in range(4):
            second[k][n][2].wait_recv()
            second[k][n][3].wait_recv()
        for g in range(4 * k, 4 * k + 4):
            rm[:, fourth(g)] = unpack_fourth(*[rm[:, packed(g, m)].astype(F32) for m in range(3)]).astype(BF16)
        lax.fori_loop(0, I // 16, lambda b, _: mix(k, b), 0, unroll=3)

    def a2a_copy(t):
        to = lax.rem(c + 1 + t, COLS)
        return pltpu.make_async_remote_copy(
            src_ref=obuf.at[pl.ds(to * IB, IB)], dst_ref=out_ref.at[:, pl.ds(pl.multiple_of(c * J, J), J), :],
            send_sem=a2a_s.at[t], recv_sem=a2a_r.at[t], device_id=(r, to), device_id_type=MESH)

    def own_copy():
        return pltpu.make_async_copy(
            obuf.at[pl.ds(c * IB, IB)], out_ref.at[:, pl.ds(pl.multiple_of(c * J, J), J), :],
            a2a_s.at[COLS - 1])

    def block(t, _):
        ib = lax.rem(c + 1 + t, COLS)
        i0 = ib * IB
        here_l = pl.ds(pl.multiple_of(i0 * JP, IB * JP), IB * JP)
        mid = ct[:, here_l].astype(F32)
        center = mid - jnp.mean(mid, axis=0, keepdims=True)
        inv = lax.rsqrt(jnp.mean(center * center, axis=0, keepdims=True) + EPS)
        xn = center * inv
        pre = dot(et[...], xn.astype(BF16))
        hgr = hgs[:, here_l].astype(F32)
        sg = 0.5 * jnp.tanh(0.5 * pre) + 0.5
        hid = pre * sg
        pgr = (hgr * (sg + hid * (1.0 - sg))).astype(BF16)
        outb = (mid + dot(st[...], hid.astype(BF16))).astype(BF16)
        hatg = dot(e_ref[...], pgr)
        m1 = jnp.mean(hatg, axis=0, keepdims=True)
        m2 = jnp.mean(hatg * xn, axis=0, keepdims=True)
        gb = (lot[:, here_l].astype(F32) + (hatg - m1 - xn * m2) * inv).astype(BF16)
        for i in range(IB):
            sl = slice(i * JP, (i + 1) * JP)
            obuf[i0 + i] = outb[:, sl].T[0:J]
            gbuf[i0 + i] = gb[:, sl].T[0:J]
        og = dot(wf[...], gb).astype(BF16)
        for i in range(IB):
            to = pl.ds(pl.multiple_of((i0 + i) * Q, Q), Q)
            for k in range(Q):
                ogs[to, k * 128:(k + 1) * 128] = og[k * Q:(k + 1) * Q, i * JP:(i + 1) * JP]

        @pl.when(t < COLS - 1)
        def _():
            a2a_copy(t).start()

        @pl.when(t == COLS - 1)
        def _():
            own_copy().start()

        return 0

    lax.fori_loop(0, COLS, block, 0, unroll=2)
    keep = pltpu.make_async_copy(gbuf, grad_hbm, io_s.at[2])
    keep.start()

    big = [[scatter_ring(chunk(rgp, k, k == 0, w), r_relay.at[k, n], r_main.at[k, n], along(k == 0), 5 * k + n)
            for n, w in enumerate(STEPS)] for k in range(2)]
    small = [scatter_direct(chunk(rgp, k, k == 1, 0), r_small.at[k], along(k == 1), 5 * k + 4)
             for k in range(2)]
    for g in range(0, G8, 2):
        a = dot(lall[...], ogs[:, packed(g, 0).start:packed(g + 1, 2).stop])
        b = dot(lall[...], ogs[:, fourth(g).start:fourth(g + 1).stop])
        for k in range(2):
            tiles = pack4(*[a[:, (3 * k + m) * 128:(3 * k + m + 1) * 128] for m in range(3)],
                          b[:, k * 128:(k + 1) * 128])
            for m in range(3):
                at = (3 * (g + k) + m) * 128
                rgp[:, at:at + 128] = tiles[m].astype(BF16)
        if g % 4 == 2:
            for n in range(4):
                big[g // 4][n][0].start()
                big[g // 4][n][1].start()

    def add(dst, *srcs):
        tot = dst[...].astype(F32)
        for src in srcs:
            tot = tot + src[...].astype(F32)
        dst[...] = tot.astype(BF16)

    def left_grad(k):
        lgt[:, k * S:(k + 1) * S] = dot_nt(rm[...], ogs[k * S:(k + 1) * S, :]).astype(BF16)

    def relayed(ring, sl, relay):
        ring[0].wait_recv()
        add(sl(1, 0, 1), relay.at[0])
        ring[2].start()
        ring[1].wait_recv()
        add(sl(-1, 1, 1), relay.at[1])
        ring[3].start()

    left_grad(0)
    for n, w in enumerate(STEPS):
        for k in range(2):
            relayed(big[k][n], chunk(rgp, k, k == 0, w), r_relay.at[k, n])
    for k in range(1, I * Q // S):
        left_grad(k)
    l_swap = [send(lgt.at[pl.ds(pl.multiple_of((2 * n + 1 - core) * SL, SL), SL)], l_sib.at[n],
                   sib_s.at[4 + n], sib_r.at[4 + n], sibling) for n in range(4)]
    for n in range(4):
        l_swap[n].start()
    for k in range(2):
        for n, w in enumerate(STEPS):
            big[k][n][2].wait_recv()
            big[k][n][3].wait_recv()
            add(chunk(rgp, k, k == 0, w)(0, 0, 2), r_main.at[k, n, 0], r_main.at[k, n, 1])
        for copy in small[k]:
            copy.start()
    for n in range(4):
        l_swap[n].wait_recv()
        add(lgt.at[pl.ds(pl.multiple_of((2 * n + core) * SL, SL), SL)], l_sib.at[n])
    l_back = scatter_ring(l_chunk(lgt), l_relay, l_main, to_x, 10)
    l_back[0].start()
    l_back[1].start()

    def hand_back(k):
        for copy in small[k]:
            copy.wait_recv()
        loose = [[], []]
        for g in range(4 * k, 4 * k + 4):
            tiles = []
            for m in range(3):
                at = (3 * g + m) * 128
                sl = slice(at - k * (PK // 2), at - k * (PK // 2) + 128)
                tot = rgp[here, at:at + 128].astype(F32)
                for n in range(3):
                    tot = tot + r_small[k, n, :, sl].astype(F32)
                tiles.append(tot)
            tiles.append(unpack_fourth(*tiles))
            for i in range(2):
                even, odd = tiles[2 * i], tiles[2 * i + 1]
                loose[0].append(jnp.where(ln16 < 64, even, roll(odd, 64)))
                loose[1].append(jnp.where(ln16 < 64, roll(even, 80), roll(odd, 16)))
        for n in range(2):
            for m in range(2):
                for i, tile in enumerate(squeeze(*loose[n][4 * m:4 * m + 4])):
                    rh[n, 6 * k + 3 * m + i] = tile.astype(BF16)
        for t in range(2):
            hop_start(*back_out(k, t))

    hand_back(0)
    relayed(l_back, l_chunk(lgt), l_relay)
    hand_back(1)
    l_back[2].wait_recv()
    l_back[3].wait_recv()
    ltot_ref[...] = (lgt[mine, :].astype(F32) + l_main[0].astype(F32) + l_main[1].astype(F32)).astype(BF16)
    for k in range(2):
        for t in range(2):
            hop_wait(*back_in(k, t))
    for m in range(4):
        dense = [jnp.concatenate([rhin[0, 3 * m + k], rhin[1, 3 * m + k]], axis=0).astype(F32) for k in range(3)]
        for k, both in enumerate(restore(*dense)):
            qp = 4 * m + k
            tq[pl.ds(2 * qp, SL, stride=Q), :] = both
            tq[pl.ds(2 * qp + 1, SL, stride=Q), :] = roll(both, 64)
    tq_ref[...] = tq[...].astype(BF16)

    def drain(t, _):
        a2a_copy(t).wait()
        return 0

    lax.fori_loop(0, COLS - 1, drain, 0)
    for ring in first + second[0] + second[1] + big[0] + big[1] + small + [l_ring, l_back, l_sibs, l_swap]:
        for copy in ring:
            copy.wait_send()
    own_copy().wait()
    keep.wait()
    for k in range(2):
        for t in range(2):
            hop_sent(*hop_out(k, t))
            hop_sent(*back_out(k, t))


def finish_kernel(out_in, grad_in, x_in, f_ref, g_ref, ltot_in, tq_in, out_ref, grad_ref, slope_ref,
                  hg, out_v, grad_v, x_ref, ltot_ref, tq_ref, sem):
    fetch = [pltpu.make_async_copy(src, dst, sem.at[k]) for k, (src, dst) in enumerate(
        ((ltot_in, ltot_ref), (tq_in, tq_ref), (x_in, x_ref), (out_in, out_v), (grad_in, grad_v)))]
    for copy in fetch:
        copy.start()
    copies = [pltpu.make_async_copy(out_v, out_ref, sem.at[5]), pltpu.make_async_copy(grad_v, grad_ref, sem.at[6])]
    f4t = dot(tile_rows(), f_ref[...]).astype(BF16)
    g4t = dot(tile_rows(), g_ref[...]).astype(BF16)
    ln = lanes((SL, 128))
    fetch[0].wait()
    for g in range(I // 4):
        tot = ltot_ref[:, g * 128:(g + 1) * 128].astype(F32)
        rows4 = jnp.concatenate(
            [jnp.where(jnp.logical_and(ln >= 32 * a, ln < 32 * a + 32), tot, 0.0) for a in range(4)], axis=0)
        res = dot(rows4.astype(BF16), f4t)
        for a in range(4):
            for k in range(2):
                hg[k, pl.ds(4 * g + a, SL, stride=I), :] = res[a * SL:(a + 1) * SL, k * 128:(k + 1) * 128]
    iden_i = eye(I, 128)
    lni = lanes((I, 128))
    for copy in fetch[1:]:
        copy.wait()
    for copy in copies:
        copy.start()

    def finish(b, _):
        rows = 4 * I
        at = pl.multiple_of(b * rows, rows)
        tj = dot_nt(iden_i, tq_ref[pl.ds(pl.multiple_of(b * 128, 128), 128), :])
        parts = [jnp.where(jnp.logical_and(lni >= 32 * a, lni < 32 * a + 32), tj, 0.0) for a in range(4)]
        right = dot(jnp.concatenate(parts, axis=0).astype(BF16), g4t)
        left = jnp.concatenate([hg[0, pl.ds(at, rows), :], hg[1, pl.ds(at, rows), :]], axis=1)
        grad = (left + right) * (1.0 / S)
        xn, inv = normalise(x_ref, b)
        m1 = jnp.mean(grad, axis=-1, keepdims=True)
        m2 = jnp.mean(grad * xn, axis=-1, keepdims=True)
        res = (grad - m1 - xn * m2) * inv
        slope_ref[pl.ds(b * 4, 4)] = res.astype(BF16).reshape(4, I, CH)
        return 0

    lax.fori_loop(0, SL // 4, finish, 0, unroll=4)
    for copy in copies:
        copy.wait()


def on_device(profile, pair, loss, former, latter, mixing, expand, shrink):
    vmem = pl.BlockSpec(memory_space=pltpu.VMEM)
    dma = pltpu.SemaphoreType.DMA
    anywhere = pl.BlockSpec(memory_space=pl.ANY)
    ft, gt = former.T, latter.T
    out, grad, ltot, tq = pl.pallas_call(
        kernel,
        out_shape=(
            jax.ShapeDtypeStruct((IB, J * COLS, C), BF16),
            jax.ShapeDtypeStruct((I, J, C), BF16),
            jax.ShapeDtypeStruct((SL, I * Q), BF16),
            jax.ShapeDtypeStruct((SL * Q, 128), BF16),
        ),
        in_specs=[vmem, anywhere, anywhere] + [vmem] * 5,
        out_specs=(anywhere, anywhere, vmem, vmem),
        scratch_shapes=[
            pltpu.VMEM((I, J, C), BF16),
            pltpu.VMEM((I, J, C), BF16),
            pltpu.VMEM((I, J, C), BF16),
            pltpu.VMEM((SL * I, 128), F32),
            pltpu.VMEM((SL * Q, 128), F32),
            pltpu.VMEM((S, I * Q), BF16),
            pltpu.VMEM((I * Q, S), BF16),
            pltpu.VMEM((12, SL, 128), BF16),
            pltpu.VMEM((2, 12, SK, 128), BF16),
            pltpu.VMEM((S, FULL), BF16),
            pltpu.VMEM((2, Q * Q // 2, 8 * JP), BF16),
            pltpu.VMEM((C, I * JP), F32),
            pltpu.VMEM((I * Q, FULL), BF16),
            pltpu.VMEM((I, J, C), BF16),
            pltpu.VMEM((Q * Q, C), F32),
            pltpu.VMEM((Q * Q, C), BF16),
            pltpu.VMEM((C, Q * Q), BF16),
            pltpu.VMEM((H, C), BF16),
            pltpu.VMEM((C, H), BF16),
            pltpu.VMEM((S, I * Q), BF16),
            pltpu.VMEM((S, PK), BF16),
            pltpu.VMEM((2, 12, SK, 128), BF16),
            pltpu.VMEM((2, 12, SK, 128), BF16),
            pltpu.VMEM((C, I * JP), BF16),
            pltpu.VMEM((C, I * JP), BF16),
            pltpu.VMEM((H, I * JP), BF16),
            pltpu.VMEM((2, 4, 2, SK, PK // 4), BF16),
            pltpu.VMEM((2, 4, 2, SK, PK // 2), BF16),
            pltpu.VMEM((2, 3, SK, PK // 2), BF16),
            pltpu.VMEM((2, SL, I * Q // 2), BF16),
            pltpu.VMEM((2, SL, I * Q), BF16),
            pltpu.VMEM((4, SL, I * Q), BF16),
            dma((3,)),
            dma((2, 2)), dma((2, 2)),
            dma((11, 4)), dma((11, 4)),
            dma((8,)), dma((8,)),
            dma((COLS,)), dma((COLS,)),
            dma((11, 4)), dma((11, 4)),
            dma((2, 2)), dma((2, 2)),
        ],
        compiler_params=pltpu.CompilerParams(
            collective_id=0, has_side_effects=True, vmem_limit_bytes=60 * 1024 * 1024),
        cost_estimate=pl.CostEstimate(flops=16_000_000_000, bytes_accessed=8_000_000, transcendentals=3_000_000),
    )(profile, pair, loss, ft, gt, mixing, expand, shrink)
    return pl.pallas_call(
        finish_kernel,
        out_shape=(
            jax.ShapeDtypeStruct((IB, J * COLS, C), BF16),
            jax.ShapeDtypeStruct((I, J, C), BF16),
            jax.ShapeDtypeStruct((SL, I, CH), BF16),
        ),
        in_specs=[anywhere, anywhere, anywhere, vmem, vmem, anywhere, anywhere],
        out_specs=(anywhere, anywhere, vmem),
        scratch_shapes=[
            pltpu.VMEM((2, SL * I, 128), F32),
            pltpu.VMEM((IB, J * COLS, C), BF16),
            pltpu.VMEM((I, J, C), BF16),
            pltpu.VMEM((SL, I, CH), BF16),
            pltpu.VMEM((SL, I * Q), BF16),
            pltpu.VMEM((SL * Q, 128), BF16),
            dma((7,)),
        ],
        compiler_params=pltpu.CompilerParams(vmem_limit_bytes=60 * 1024 * 1024),
        cost_estimate=pl.CostEstimate(flops=400_000_000, bytes_accessed=6_000_000, transcendentals=2_000),
    )(out, grad, profile, ft, gt, ltot, tq)


def solution(mesh):
    return jax.shard_map(
        on_device,
        mesh=mesh,
        in_specs=(P("col", "row", None), P("row", "col", None), P("row", "col", None), P(), P(), P(), P(), P()),
        out_specs=(P(("row", "col"), None, None), P("row", "col", None), P("col", "row", None)),
        check_vma=False,
    )
```

```python
import functools

import jax
import jax.numpy as jnp
from jax import lax
from jax.experimental import pallas as pl
from jax.experimental.pallas import tpu as pltpu
from jax.sharding import PartitionSpec as P

MESH = pl.DeviceIdType.MESH
EPS = 1e-05
F32 = jnp.float32
BF16 = jnp.bfloat16

ROWS, COLS = 16, 8
S, SL = 256, 32
I, J, JP = 48, 96, 128
Q = 32
C, H, CH = 128, 512, 256
SK = S // ROWS
G8 = Q // 4
PK = 3 * G8 * 128
FULL = Q * JP
IB = I // COLS
HALF = FULL // 2
SLABS = sum(([4 * g + m for g in range(4 * k, 4 * k + 4) for m in range(3)]
             + [4 * g + 3 for g in range(4 * k, 4 * k + 4)] for k in range(2)), [])


def packed(g, m):
    at = (g // 4) * HALF + (3 * (g % 4) + m) * 128
    return slice(at, at + 128)


def fourth(g):
    at = (g // 4) * HALF + (12 + g % 4) * 128
    return slice(at, at + 128)


def dot(a, b):
    return jnp.dot(a, b, preferred_element_type=F32)


def dot_nt(a, b):
    return lax.dot_general(a, b, (((1,), (1,)), ((), ())), preferred_element_type=F32)


def eye(n, m=None):
    m = n if m is None else m
    i = lax.broadcasted_iota(jnp.int32, (n, m), 0)
    j = lax.broadcasted_iota(jnp.int32, (n, m), 1)
    return jnp.where(i == j, 1.0, 0.0).astype(BF16)


def lanes(shape):
    return lax.broadcasted_iota(jnp.int32, shape, 1)


def roll(x, shift):
    return pltpu.roll(x, shift, 1)


def pack4(q0, q1, q2, q3):
    ln = lanes(q0.shape)
    return (
        jnp.where(ln < 96, q0, roll(q3, 96)),
        jnp.where(ln < 96, q1, roll(q3, 64)),
        jnp.where(ln < 96, q2, roll(q3, 32)),
    )


def squeeze(t0, t1, t2, t3):
    inner = lax.rem(lanes(t0.shape), 64)
    return [jnp.where(inner < 48, t, roll(t3, 48 - 16 * k)) for k, t in enumerate((t0, t1, t2))]


def restore(t0, t1, t2):
    inner = lax.rem(lanes(t0.shape), 64)
    return [t0, t1, t2, jnp.where(inner < 16, roll(t0, 80), jnp.where(inner < 32, roll(t1, 96), roll(t2, 112)))]


def unpack_fourth(t0, t1, t2):
    ln = lanes(t0.shape)
    return jnp.where(ln < 32, roll(t0, 32), jnp.where(ln < 64, roll(t1, 64), roll(t2, 96)))


def tile_rows():
    return jnp.where(
        lax.rem(lax.broadcasted_iota(jnp.int32, (128, Q), 0), Q)
        == lax.broadcasted_iota(jnp.int32, (128, Q), 1), 1.0, 0.0).astype(BF16)


def normalise(x_ref, b):
    xr = x_ref[pl.ds(b * 4, 4)].reshape(4 * I, CH).astype(F32)
    center = xr - jnp.mean(xr, axis=-1, keepdims=True)
    inv = lax.rsqrt(jnp.mean(center * center, axis=-1, keepdims=True) + EPS)
    return center * inv, inv


def kernel(
    x_ref, pair_hbm, loss_hbm, f_ref, g_ref, w_ref, e_ref, s_ref,
    out_ref, grad_hbm, ltot_ref, tq_ref,
    pair_ref, loss_ref, gbuf, proj, tq, lall, lt, rhop, rin, rm, xs, acc, ogs, obuf,
    wf32, wf, wt, et, st, lgt, rgp, rh, rhin, ct, lot, hgs, r_relay, r_main, r_small, l_relay, l_main, l_sib,
    io_s, hop_s, hop_r, ag_s, ag_r, sib_s, sib_r, a2a_s, a2a_r, rs_s, rs_r, hop2_s, hop2_r,
):
    r = lax.axis_index("row")
    c = lax.axis_index("col")
    half = lax.rem(r, 2)
    across = lax.div(r, 2)

    z, y = lax.div(r, 4), lax.rem(r, 4)
    fetch = [pltpu.make_async_copy(pair_hbm, pair_ref, io_s.at[0]), pltpu.make_async_copy(loss_hbm, loss_ref, io_s.at[1])]
    for copy in fetch:
        copy.start()
    x, core = lax.div(c, 2), lax.rem(c, 2)

    barrier = pltpu.get_barrier_semaphore()

    def at_row(z_, y_):
        return 4 * lax.rem(z_ + 4, 4) + lax.rem(y_ + 4, 4)

    def at_col(x_):
        return 2 * lax.rem(x_ + 4, 4) + core

    for row in (at_row(z - 1, y), at_row(z + 1, y), at_row(z + 2, y), at_row(z, y - 1), at_row(z, y + 1), at_row(z, y + 2)):
        pl.semaphore_signal(barrier, inc=1, device_id=(row, c), device_id_type=MESH)

    def greet_col(d, _):
        pl.semaphore_signal(barrier, inc=1, device_id=(r, lax.rem(c + d, COLS)), device_id_type=MESH)
        return 0

    lax.fori_loop(1, COLS, greet_col, 0)
    own = [jnp.logical_and(across == c, half == t) for t in range(2)]
    for t in range(2):
        @pl.when(jnp.logical_not(own[t]))
        def _():
            pl.semaphore_signal(barrier, inc=1, device_id=(2 * c + t, across), device_id_type=MESH)

    iden = eye(C)
    ln128 = lanes((SL, 128))
    f4t = dot(tile_rows(), f_ref[...]).astype(BF16)
    tq[...] = jnp.zeros_like(tq)

    def project(b, _):
        rows = 4 * I
        at = pl.multiple_of(b * rows, rows)
        xn = normalise(x_ref, b)[0]
        xb = xn.astype(BF16)
        proj[pl.ds(at, rows), :] = dot_nt(xb, f4t)
        for k in range(4):
            to = pl.multiple_of((b * 4 + k) * Q, Q)
            tq[pl.ds(to, Q), 0:I] = dot_nt(g_ref[...], xb[k * I:(k + 1) * I])
        return 0

    lax.fori_loop(0, SL // 4, project, 0, unroll=4)

    mine = pl.ds(pl.multiple_of(c * SL, SL), SL)
    for m in range(4):
        pairs = []
        for qp in range(4 * m, 4 * m + 4):
            even = tq[pl.ds(2 * qp, SL, stride=Q), :]
            odd = tq[pl.ds(2 * qp + 1, SL, stride=Q), :]
            pairs.append(jnp.where(ln128 < 64, even, roll(odd, 64)))
        for k, tile in enumerate(squeeze(*pairs)):
            rhop[3 * m + k] = tile.astype(BF16)
    for g in range(I // 4):
        parts = [proj[pl.ds(4 * g + a, SL, stride=I), :] for a in range(4)]
        tile = jnp.where(ln128 < 32, parts[0], jnp.where(ln128 < 64, parts[1],
                         jnp.where(ln128 < 96, parts[2], parts[3])))
        lall[mine, g * 128:(g + 1) * 128] = tile.astype(BF16)

    pl.semaphore_wait(barrier, 6 + COLS - 1 + 2 - (across == c).astype(jnp.int32))

    def hop_remote(src, dst, t, ss, rs):
        return pltpu.make_async_remote_copy(
            src_ref=src, dst_ref=dst, send_sem=ss, recv_sem=rs,
            device_id=(2 * c + t, across), device_id_type=MESH)

    def hop_start(src, dst, t, ss, rs):
        @pl.when(own[t])
        def _():
            pltpu.make_async_copy(src, dst, rs).start()

        @pl.when(jnp.logical_not(own[t]))
        def _():
            hop_remote(src, dst, t, ss, rs).start()

    def hop_wait(src, dst, t, ss, rs):
        @pl.when(own[t])
        def _():
            pltpu.make_async_copy(src, dst, rs).wait()

        @pl.when(jnp.logical_not(own[t]))
        def _():
            hop_remote(src, dst, t, ss, rs).wait_recv()

    def hop_sent(src, dst, t, ss, rs):
        @pl.when(jnp.logical_not(own[t]))
        def _():
            hop_remote(src, dst, t, ss, rs).wait_send()

    def hop_out(k, t):
        return (rhop.at[pl.ds(6 * k, 6), pl.ds(SK * t, SK), :], rin.at[half, pl.ds(6 * k, 6)], t,
                hop_s.at[k, t], hop_r.at[k, half])

    def hop_in(k, t):
        return (rhop.at[pl.ds(6 * k, 6), pl.ds(SK * t, SK), :], rin.at[t, pl.ds(6 * k, 6)], t,
                hop_s.at[k, t], hop_r.at[k, t])

    def back_out(k, t):
        return (rh.at[t, pl.ds(6 * k, 6)], rhin.at[half, pl.ds(6 * k, 6)], t, hop2_s.at[k, t], hop2_r.at[k, half])

    def back_in(k, t):
        return (rh.at[t, pl.ds(6 * k, 6)], rhin.at[t, pl.ds(6 * k, 6)], t, hop2_s.at[k, t], hop2_r.at[k, t])

    for k in range(2):
        for t in range(2):
            hop_start(*hop_out(k, t))

    wf32[...] = w_ref[...].astype(F32)
    for k, q in enumerate(SLABS):
        wf[k * Q:(k + 1) * Q, :] = wf32[pl.ds(q, Q, stride=Q), :].astype(BF16)
    wt[...] = dot_nt(iden, wf[...]).astype(BF16)
    st[...] = dot_nt(iden, s_ref[...]).astype(BF16)
    et[...] = dot_nt(eye(H), e_ref[...]).astype(BF16)
    pad = jnp.zeros((JP - J, C), BF16)
    for copy in fetch:
        copy.wait()

    def ahead(k, _):
        to = pl.ds(pl.multiple_of(k * 256, 256), 256)
        pr = jnp.concatenate([pair_ref[2 * k], pad, pair_ref[2 * k + 1], pad], axis=0)
        lo = jnp.concatenate([loss_ref[2 * k], pad, loss_ref[2 * k + 1], pad], axis=0)
        ct[:, to] = pr.T
        lob = lo.T
        lot[:, to] = lob
        hgs[:, to] = dot(s_ref[...], lob).astype(BF16)
        return 0

    lax.fori_loop(0, 24, ahead, 0, unroll=6)

    ln16 = lanes((SK, 128))
    here = pl.ds(pl.multiple_of(r * SK, SK), SK)

    def assemble(k):
        loose = [sum((restore(*[rin[n, 3 * m + i].astype(F32) for i in range(3)]) for m in (2 * k, 2 * k + 1)), [])
                 for n in range(2)]
        for g in range(4):
            tiles = []
            for i in range(2):
                a, b = loose[0][2 * g + i], loose[1][2 * g + i]
                tiles.append(jnp.where(ln16 < 48, a, roll(b, 48)))
                tiles.append(jnp.where(ln16 < 48, roll(a, 64), roll(b, 112)))
            for m, tile in enumerate(pack4(*tiles)):
                rm[here, packed(4 * k + g, m)] = tile.astype(BF16)

    def send(src, dst, ss, rs, to):
        return pltpu.make_async_remote_copy(
            src_ref=src, dst_ref=dst, send_sem=ss, recv_sem=rs, device_id=to, device_id_type=MESH)

    def gather_ring(sl, to, g):
        return [
            send(sl(0, 0, 2), sl(0, 0, 2), ag_s.at[g, 0], ag_r.at[g, 0], to(1)),
            send(sl(0, 0, 2), sl(0, 0, 2), ag_s.at[g, 1], ag_r.at[g, 1], to(-1)),
            send(sl(-1, 0, 1), sl(-1, 0, 1), ag_s.at[g, 2], ag_r.at[g, 2], to(1)),
            send(sl(1, 1, 1), sl(1, 1, 1), ag_s.at[g, 3], ag_r.at[g, 3], to(-1)),
        ]

    def gather_direct(sl, to, g):
        return [send(sl(0, 0, 2), sl(0, 0, 2), ag_s.at[g, k], ag_r.at[g, k], to(d)) for k, d in enumerate((1, -1, 2))]

    def scatter_direct(sl, into, to, g):
        return [send(sl(d, 0, 2), into.at[k], rs_s.at[g, k], rs_r.at[g, k], to(d)) for k, d in enumerate((1, -1, 2))]

    def scatter_ring(sl, relay, main, to, g):
        return [
            send(sl(2, 0, 1), relay.at[0], rs_s.at[g, 0], rs_r.at[g, 0], to(1)),
            send(sl(2, 1, 1), relay.at[1], rs_s.at[g, 1], rs_r.at[g, 1], to(-1)),
            send(sl(1, 0, 2), main.at[0], rs_s.at[g, 2], rs_r.at[g, 2], to(1)),
            send(sl(-1, 0, 2), main.at[1], rs_s.at[g, 3], rs_r.at[g, 3], to(-1)),
        ]

    def chunk(ref, side, along_z, w):
        def sl(off, first, count):
            row = at_row(z + off, y + w) if along_z else at_row(z + w, y + off)
            return ref.at[pl.ds(pl.multiple_of(row * SK, SK), SK),
                          pl.ds(side * (HALF if ref is rm else PK // 2) + first * (PK // 4), count * (PK // 4))]
        return sl

    def along(along_z):
        return lambda d: (at_row(z + d, y), c) if along_z else (at_row(z, y + d), c)

    def l_chunk(ref):
        def sl(off, first, count):
            return ref.at[pl.ds(pl.multiple_of(at_col(x + off) * SL, SL), SL), pl.ds(first * (I * Q // 2), count * (I * Q // 2))]
        return sl

    def to_x(d):
        return (r, at_col(x + d))

    sibling = (r, c + 1 - 2 * core)
    STEPS = (0, -1, 1, 2)
    first = [gather_direct(chunk(rm, k, k == 1, 0), along(k == 1), 5 * k) for k in range(2)]
    second = [[gather_ring(chunk(rm, k, k == 0, w), along(k == 0), 5 * k + 1 + n)
               for n, w in enumerate(STEPS)] for k in range(2)]
    l_ring = gather_ring(l_chunk(lall), to_x, 10)
    l_sibs = [send(l_chunk(lall)(w, 0, 2), l_chunk(lall)(w, 0, 2), sib_s.at[n], sib_r.at[n], sibling)
              for n, w in enumerate(STEPS)]
    for k in range(2):
        for t in range(2):
            hop_wait(*hop_in(k, t))
        assemble(k)
        for copy in first[k] + second[k][0][:2]:
            copy.start()
    l_ring[0].start()
    l_ring[1].start()
    l_sibs[0].start()
    for k in range(2):
        for m in range(3):
            first[k][m].wait_recv()
            second[k][1 + m][0].start()
            second[k][1 + m][1].start()
    for m in range(2):
        l_ring[m].wait_recv()
        l_ring[2 + m].start()
        l_sibs[1 + m].start()
    for k in range(2):
        for n in range(4):
            for m in range(2):
                second[k][n][m].wait_recv()
                second[k][n][2 + m].start()
    l_ring[2].wait_recv()
    l_ring[3].wait_recv()
    l_sibs[3].start()
    for n in range(4):
        l_sibs[n].wait_recv()
    for k in range(I * Q // S):
        lt[k * S:(k + 1) * S, :] = lall[:, k * S:(k + 1) * S].T
    scale = 1.0 / S

    def mix(side, b):
        for k in range(2):
            at = pl.multiple_of((2 * b + k) * 256, 256)
            ltb = lt[pl.ds(at, 256), :]
            for ch in range(4):
                d = dot(ltb, rm[:, side * HALF + ch * 512:side * HALF + (ch + 1) * 512]).astype(BF16)
                for m in range(4):
                    slab = ch * 4 + m
                    for i in range(8):
                        xs[k, slab * Q:(slab + 1) * Q, i * JP:(i + 1) * JP] = d[i * Q:(i + 1) * Q, m * 128:(m + 1) * 128]
        for k in range(2):
            to = pl.ds(pl.multiple_of((2 * b + k) * 1024, 1024), 1024)
            part = dot(wt[:, side * 512:(side + 1) * 512], xs[k])
            if side == 0:
                acc[:, to] = part
            else:
                ct[:, to] = (ct[:, to].astype(F32) + (acc[:, to] + part) * scale).astype(BF16)
        return 0

    for k in range(2):
        for n in range(4):
            second[k][n][2].wait_recv()
            second[k][n][3].wait_recv()
        for g in range(4 * k, 4 * k + 4):
            rm[:, fourth(g)] = unpack_fourth(*[rm[:, packed(g, m)].astype(F32) for m in range(3)]).astype(BF16)
        lax.fori_loop(0, I // 16, lambda b, _: mix(k, b), 0, unroll=3)

    def a2a_copy(t):
        to = lax.rem(c + 1 + t, COLS)
        return pltpu.make_async_remote_copy(
            src_ref=obuf.at[pl.ds(to * IB, IB)], dst_ref=out_ref.at[:, pl.ds(pl.multiple_of(c * J, J), J), :],
            send_sem=a2a_s.at[t], recv_sem=a2a_r.at[t], device_id=(r, to), device_id_type=MESH)

    def own_copy():
        return pltpu.make_async_copy(
            obuf.at[pl.ds(c * IB, IB)], out_ref.at[:, pl.ds(pl.multiple_of(c * J, J), J), :],
            a2a_s.at[COLS - 1])

    def block(t, _):
        ib = lax.rem(c + 1 + t, COLS)
        i0 = ib * IB
        here_l = pl.ds(pl.multiple_of(i0 * JP, IB * JP), IB * JP)
        mid = ct[:, here_l].astype(F32)
        center = mid - jnp.mean(mid, axis=0, keepdims=True)
        inv = lax.rsqrt(jnp.mean(center * center, axis=0, keepdims=True) + EPS)
        xn = center * inv
        pre = dot(et[...], xn.astype(BF16))
        hgr = hgs[:, here_l].astype(F32)
        sg = 0.5 * jnp.tanh(0.5 * pre) + 0.5
        hid = pre * sg
        pgr = (hgr * (sg + hid * (1.0 - sg))).astype(BF16)
        outb = (mid + dot(st[...], hid.astype(BF16))).astype(BF16)
        hatg = dot(e_ref[...], pgr)
        m1 = jnp.mean(hatg, axis=0, keepdims=True)
        m2 = jnp.mean(hatg * xn, axis=0, keepdims=True)
        gb = (lot[:, here_l].astype(F32) + (hatg - m1 - xn * m2) * inv).astype(BF16)
        for i in range(IB):
            sl = slice(i * JP, (i + 1) * JP)
            obuf[i0 + i] = outb[:, sl].T[0:J]
            gbuf[i0 + i] = gb[:, sl].T[0:J]
        og = dot(wf[...], gb).astype(BF16)
        for i in range(IB):
            to = pl.ds(pl.multiple_of((i0 + i) * Q, Q), Q)
            for k in range(Q):
                ogs[to, k * 128:(k + 1) * 128] = og[k * Q:(k + 1) * Q, i * JP:(i + 1) * JP]

        @pl.when(t < COLS - 1)
        def _():
            a2a_copy(t).start()

        @pl.when(t == COLS - 1)
        def _():
            own_copy().start()

        return 0

    lax.fori_loop(0, COLS, block, 0, unroll=2)
    keep = pltpu.make_async_copy(gbuf, grad_hbm, io_s.at[2])
    keep.start()

    big = [[scatter_ring(chunk(rgp, k, k == 0, w), r_relay.at[k, n], r_main.at[k, n], along(k == 0), 5 * k + n)
            for n, w in enumerate(STEPS)] for k in range(2)]
    small = [scatter_direct(chunk(rgp, k, k == 1, 0), r_small.at[k], along(k == 1), 5 * k + 4)
             for k in range(2)]
    for g in range(0, G8, 2):
        a = dot(lall[...], ogs[:, packed(g, 0).start:packed(g + 1, 2).stop])
        b = dot(lall[...], ogs[:, fourth(g).start:fourth(g + 1).stop])
        for k in range(2):
            tiles = pack4(*[a[:, (3 * k + m) * 128:(3 * k + m + 1) * 128] for m in range(3)],
                          b[:, k * 128:(k + 1) * 128])
            for m in range(3):
                at = (3 * (g + k) + m) * 128
                rgp[:, at:at + 128] = tiles[m].astype(BF16)
        if g % 4 == 2:
            for n in range(4):
                big[g // 4][n][0].start()
                big[g // 4][n][1].start()

    def add(dst, *srcs):
        tot = dst[...].astype(F32)
        for src in srcs:
            tot = tot + src[...].astype(F32)
        dst[...] = tot.astype(BF16)

    def left_grad(k):
        lgt[:, k * S:(k + 1) * S] = dot_nt(rm[...], ogs[k * S:(k + 1) * S, :]).astype(BF16)

    def relayed(ring, sl, relay):
        ring[0].wait_recv()
        add(sl(1, 0, 1), relay.at[0])
        ring[2].start()
        ring[1].wait_recv()
        add(sl(-1, 1, 1), relay.at[1])
        ring[3].start()

    left_grad(0)
    for k in range(2):
        for n, w in enumerate(STEPS):
            relayed(big[k][n], chunk(rgp, k, k == 0, w), r_relay.at[k, n])
    for k in range(1, I * Q // S):
        left_grad(k)
    l_swap = [send(lgt.at[pl.ds(pl.multiple_of((2 * n + 1 - core) * SL, SL), SL)], l_sib.at[n],
                   sib_s.at[4 + n], sib_r.at[4 + n], sibling) for n in range(4)]
    for n in range(4):
        l_swap[n].start()
    for k in range(2):
        for n, w in enumerate(STEPS):
            big[k][n][2].wait_recv()
            big[k][n][3].wait_recv()
            add(chunk(rgp, k, k == 0, w)(0, 0, 2), r_main.at[k, n, 0], r_main.at[k, n, 1])
        for copy in small[k]:
            copy.start()
    for n in range(4):
        l_swap[n].wait_recv()
        add(lgt.at[pl.ds(pl.multiple_of((2 * n + core) * SL, SL), SL)], l_sib.at[n])
    l_back = scatter_ring(l_chunk(lgt), l_relay, l_main, to_x, 10)
    l_back[0].start()
    l_back[1].start()

    def hand_back(k):
        for copy in small[k]:
            copy.wait_recv()
        loose = [[], []]
        for g in range(4 * k, 4 * k + 4):
            tiles = []
            for m in range(3):
                at = (3 * g + m) * 128
                sl = slice(at - k * (PK // 2), at - k * (PK // 2) + 128)
                tot = rgp[here, at:at + 128].astype(F32)
                for n in range(3):
                    tot = tot + r_small[k, n, :, sl].astype(F32)
                tiles.append(tot)
            tiles.append(unpack_fourth(*tiles))
            for i in range(2):
                even, odd = tiles[2 * i], tiles[2 * i + 1]
                loose[0].append(jnp.where(ln16 < 64, even, roll(odd, 64)))
                loose[1].append(jnp.where(ln16 < 64, roll(even, 80), roll(odd, 16)))
        for n in range(2):
            for m in range(2):
                for i, tile in enumerate(squeeze(*loose[n][4 * m:4 * m + 4])):
                    rh[n, 6 * k + 3 * m + i] = tile.astype(BF16)
        for t in range(2):
            hop_start(*back_out(k, t))

    hand_back(0)
    relayed(l_back, l_chunk(lgt), l_relay)
    hand_back(1)
    l_back[2].wait_recv()
    l_back[3].wait_recv()
    ltot_ref[...] = (lgt[mine, :].astype(F32) + l_main[0].astype(F32) + l_main[1].astype(F32)).astype(BF16)
    for k in range(2):
        for t in range(2):
            hop_wait(*back_in(k, t))
    for m in range(4):
        dense = [jnp.concatenate([rhin[0, 3 * m + k], rhin[1, 3 * m + k]], axis=0).astype(F32) for k in range(3)]
        for k, both in enumerate(restore(*dense)):
            qp = 4 * m + k
            tq[pl.ds(2 * qp, SL, stride=Q), :] = both
            tq[pl.ds(2 * qp + 1, SL, stride=Q), :] = roll(both, 64)
    tq_ref[...] = tq[...].astype(BF16)

    def drain(t, _):
        a2a_copy(t).wait()
        return 0

    lax.fori_loop(0, COLS - 1, drain, 0)
    for ring in first + second[0] + second[1] + big[0] + big[1] + small + [l_ring, l_back, l_sibs, l_swap]:
        for copy in ring:
            copy.wait_send()
    own_copy().wait()
    keep.wait()
    for k in range(2):
        for t in range(2):
            hop_sent(*hop_out(k, t))
            hop_sent(*back_out(k, t))


def finish_kernel(out_in, grad_in, x_in, f_ref, g_ref, ltot_in, tq_in, out_ref, grad_ref, slope_ref,
                  hg, out_v, grad_v, x_ref, ltot_ref, tq_ref, sem):
    fetch = [pltpu.make_async_copy(src, dst, sem.at[k]) for k, (src, dst) in enumerate(
        ((ltot_in, ltot_ref), (tq_in, tq_ref), (x_in, x_ref), (out_in, out_v), (grad_in, grad_v)))]
    for copy in fetch:
        copy.start()
    copies = [pltpu.make_async_copy(out_v, out_ref, sem.at[5]), pltpu.make_async_copy(grad_v, grad_ref, sem.at[6])]
    f4t = dot(tile_rows(), f_ref[...]).astype(BF16)
    g4t = dot(tile_rows(), g_ref[...]).astype(BF16)
    ln = lanes((SL, 128))
    fetch[0].wait()
    for g in range(I // 4):
        tot = ltot_ref[:, g * 128:(g + 1) * 128].astype(F32)
        rows4 = jnp.concatenate(
            [jnp.where(jnp.logical_and(ln >= 32 * a, ln < 32 * a + 32), tot, 0.0) for a in range(4)], axis=0)
        res = dot(rows4.astype(BF16), f4t)
        for a in range(4):
            for k in range(2):
                hg[k, pl.ds(4 * g + a, SL, stride=I), :] = res[a * SL:(a + 1) * SL, k * 128:(k + 1) * 128]
    iden_i = eye(I, 128)
    lni = lanes((I, 128))
    for copy in fetch[1:]:
        copy.wait()
    for copy in copies:
        copy.start()

    def finish(b, _):
        rows = 4 * I
        at = pl.multiple_of(b * rows, rows)
        tj = dot_nt(iden_i, tq_ref[pl.ds(pl.multiple_of(b * 128, 128), 128), :])
        parts = [jnp.where(jnp.logical_and(lni >= 32 * a, lni < 32 * a + 32), tj, 0.0) for a in range(4)]
        right = dot(jnp.concatenate(parts, axis=0).astype(BF16), g4t)
        left = jnp.concatenate([hg[0, pl.ds(at, rows), :], hg[1, pl.ds(at, rows), :]], axis=1)
        grad = (left + right) * (1.0 / S)
        xn, inv = normalise(x_ref, b)
        m1 = jnp.mean(grad, axis=-1, keepdims=True)
        m2 = jnp.mean(grad * xn, axis=-1, keepdims=True)
        res = (grad - m1 - xn * m2) * inv
        slope_ref[pl.ds(b * 4, 4)] = res.astype(BF16).reshape(4, I, CH)
        return 0

    lax.fori_loop(0, SL // 4, finish, 0, unroll=4)
    for copy in copies:
        copy.wait()


def on_device(profile, pair, loss, former, latter, mixing, expand, shrink):
    vmem = pl.BlockSpec(memory_space=pltpu.VMEM)
    dma = pltpu.SemaphoreType.DMA
    anywhere = pl.BlockSpec(memory_space=pl.ANY)
    ft, gt = former.T, latter.T
    out, grad, ltot, tq = pl.pallas_call(
        kernel,
        out_shape=(
            jax.ShapeDtypeStruct((IB, J * COLS, C), BF16),
            jax.ShapeDtypeStruct((I, J, C), BF16),
            jax.ShapeDtypeStruct((SL, I * Q), BF16),
            jax.ShapeDtypeStruct((SL * Q, 128), BF16),
        ),
        in_specs=[vmem, anywhere, anywhere] + [vmem] * 5,
        out_specs=(anywhere, anywhere, vmem, vmem),
        scratch_shapes=[
            pltpu.VMEM((I, J, C), BF16),
            pltpu.VMEM((I, J, C), BF16),
            pltpu.VMEM((I, J, C), BF16),
            pltpu.VMEM((SL * I, 128), F32),
            pltpu.VMEM((SL * Q, 128), F32),
            pltpu.VMEM((S, I * Q), BF16),
            pltpu.VMEM((I * Q, S), BF16),
            pltpu.VMEM((12, SL, 128), BF16),
            pltpu.VMEM((2, 12, SK, 128), BF16),
            pltpu.VMEM((S, FULL), BF16),
            pltpu.VMEM((2, Q * Q // 2, 8 * JP), BF16),
            pltpu.VMEM((C, I * JP), F32),
            pltpu.VMEM((I * Q, FULL), BF16),
            pltpu.VMEM((I, J, C), BF16),
            pltpu.VMEM((Q * Q, C), F32),
            pltpu.VMEM((Q * Q, C), BF16),
            pltpu.VMEM((C, Q * Q), BF16),
            pltpu.VMEM((H, C), BF16),
            pltpu.VMEM((C, H), BF16),
            pltpu.VMEM((S, I * Q), BF16),
            pltpu.VMEM((S, PK), BF16),
            pltpu.VMEM((2, 12, SK, 128), BF16),
            pltpu.VMEM((2, 12, SK, 128), BF16),
            pltpu.VMEM((C, I * JP), BF16),
            pltpu.VMEM((C, I * JP), BF16),
            pltpu.VMEM((H, I * JP), BF16),
            pltpu.VMEM((2, 4, 2, SK, PK // 4), BF16),
            pltpu.VMEM((2, 4, 2, SK, PK // 2), BF16),
            pltpu.VMEM((2, 3, SK, PK // 2), BF16),
            pltpu.VMEM((2, SL, I * Q // 2), BF16),
            pltpu.VMEM((2, SL, I * Q), BF16),
            pltpu.VMEM((4, SL, I * Q), BF16),
            dma((3,)),
            dma((2, 2)), dma((2, 2)),
            dma((11, 4)), dma((11, 4)),
            dma((8,)), dma((8,)),
            dma((COLS,)), dma((COLS,)),
            dma((11, 4)), dma((11, 4)),
            dma((2, 2)), dma((2, 2)),
        ],
        compiler_params=pltpu.CompilerParams(
            collective_id=0, has_side_effects=True, vmem_limit_bytes=60 * 1024 * 1024),
        cost_estimate=pl.CostEstimate(flops=16_000_000_000, bytes_accessed=8_000_000, transcendentals=3_000_000),
    )(profile, pair, loss, ft, gt, mixing, expand, shrink)
    return pl.pallas_call(
        finish_kernel,
        out_shape=(
            jax.ShapeDtypeStruct((IB, J * COLS, C), BF16),
            jax.ShapeDtypeStruct((I, J, C), BF16),
            jax.ShapeDtypeStruct((SL, I, CH), BF16),
        ),
        in_specs=[anywhere, anywhere, anywhere, vmem, vmem, anywhere, anywhere],
        out_specs=(anywhere, anywhere, vmem),
        scratch_shapes=[
            pltpu.VMEM((2, SL * I, 128), F32),
            pltpu.VMEM((IB, J * COLS, C), BF16),
            pltpu.VMEM((I, J, C), BF16),
            pltpu.VMEM((SL, I, CH), BF16),
            pltpu.VMEM((SL, I * Q), BF16),
            pltpu.VMEM((SL * Q, 128), BF16),
            dma((7,)),
        ],
        compiler_params=pltpu.CompilerParams(vmem_limit_bytes=60 * 1024 * 1024),
        cost_estimate=pl.CostEstimate(flops=400_000_000, bytes_accessed=6_000_000, transcendentals=2_000),
    )(out, grad, profile, ft, gt, ltot, tq)


def solution(mesh):
    return jax.shard_map(
        on_device,
        mesh=mesh,
        in_specs=(P("col", "row", None), P("row", "col", None), P("row", "col", None), P(), P(), P(), P(), P()),
        out_specs=(P(("row", "col"), None, None), P("row", "col", None), P("col", "row", None)),
        check_vma=False,
    )
```
